32 devices in a mesh: gx: 4 (over z), gy: 2 (over x), gz: 4 (over y, core).
Axes of the slice: x: 2, y: 2, z: 4, core: 2. Of those that a mesh axis runs over, the one named last changes fastest.
Arguments:
- density: float32 [16, 8, 512], P('gx', 'gy', 'gz'), may hold values from 0.5 to 2
- velocity: float32 [3, 16, 8, 512], P(None, 'gx', 'gy', 'gz'), may hold values from -3 to 3
- pressure: float32 [16, 8, 512], P('gx', 'gy', 'gz'), may hold values from 0.5 to 2
- fine_density: float32 [4, 2, 8, 8, 128], P('gx', 'gy', 'gz'), may hold values from -0.2 to 0.2
- fine_velocity: float32 [3, 4, 2, 8, 8, 128], P(None, 'gx', 'gy', 'gz'), may hold values from -3 to 3
- fine_pressure: float32 [4, 2, 8, 8, 128], P('gx', 'gy', 'gz'), may hold values from -0.2 to 0.2
- box_parent: int32 [4, 2, 8, 1], P('gx', 'gy'), may hold values from 0 to 3; in each aligned block of 2 rows (0 to 1, 2 to 3, ..., all dimensions but the last counted through in order) no two rows name the same one
- box_shift: int32 [4, 2, 8], P('gx', 'gy'), may hold values from 0 to 120
Outputs:
- coarse_state: float32 [5, 16, 8, 512], P(None, 'gx', 'gy', 'gz')
- fine_state: float32 [5, 4, 2, 8, 8, 128], P(None, 'gx', 'gy', 'gz')
The draws below stay inside these ranges and needn't reach their ends.
Inputs may be any that keep to these rules, and one draw needn't show every extreme that they name: `box_parent`: among the 2 boxes of one owner (one aligned block), no parent is named more than 1 times, and in some blocks one parent is named exactly 1 times.
All inputs are finite; a program needn't handle non-finite values.
Results may differ from the reference program's by a relative error of at most 0.0003.
Values sent between devices are 32-bit elements; how exact they have to be, the bound alone decides.
A program may use at most 64 MiB of HBM per device.

```python
import math
import jax
import jax.numpy as jnp
import numpy as np
from jax import lax

CX = 4
CY = 4
CZ = 128
FZ = 16
BOX_DEV = 2
FX = 8
FY = 8
CAP = 1
BOXES = 8
NX = 16
NY = 8
NZ = 512
N_GX = 4
N_GY = 2
N_GZ = 4


def touch_ends(values, stream_key, smallest, high):
    shape = values.shape
    spot = [jax.random.randint(jax.random.fold_in(stream_key, axis), (), 0, shape[axis]) for axis in range(len(shape))]
    values = values.at[tuple(spot)].set(smallest)
    longest = shape.index(max(shape))
    spot[longest] = (spot[longest] + 1) % shape[longest]
    return values.at[tuple(spot)].set(high)


def level_of(key, shape, pieces, low, largest):
    factor_of = 1.0
    for axis_at, blocks in pieces:
        steps = jax.random.uniform(jax.random.fold_in(jax.random.fold_in(key, 6), axis_at), (blocks,), jnp.float32, low / len(pieces), largest / len(pieces))
        factor_of = factor_of * jnp.repeat(jnp.exp(steps), shape[axis_at] // blocks).reshape((-1,) + (1,) * (len(shape) - 1 - axis_at))
    return factor_of


def shared_out(rng, own, number, rows, number_of, top, bound, lean):
    sequence = jax.random.permutation(rng, number_of)
    crowded, ordinary = portions_of(number_of, rows * top, bound, lean, True), portions_of(number_of, rows * top, bound, lean, False)
    places = jnp.arange(number_of)

    def named(lengths, rotation):
        used = int((lengths > 0).sum())
        fixed = max(1, used // 4)
        passed = fixed + (places - fixed + rotation * (used - fixed)) % max(1, number_of - fixed)
        return jnp.zeros((number_of,), jnp.int32).at[sequence[jnp.where(places < fixed, places, passed)]].set(jnp.asarray(lengths, jnp.int32))

    lengths = jnp.where(number % 4 == 0, named(crowded, number // 4), named(ordinary, number - number // 4 - 1))
    mixed = jax.random.permutation(jax.random.fold_in(own, 3), number_of)
    source_of, taker = mixed[0:number_of // 2 * 2:2], mixed[1:number_of // 2 * 2:2]
    room = jnp.minimum(lengths[source_of] - 1, bound - lengths[taker]) // 2
    room = jnp.where((source_of == sequence[0]) | (taker == sequence[0]) | (lengths[taker] == 0), 0, jnp.maximum(room, 0))
    passed = jax.random.randint(jax.random.fold_in(own, 4), (number_of // 2,), 0, 1 << 20) % (room + 1)
    lengths = lengths.at[source_of].add(-passed).at[taker].add(passed)
    members = jnp.searchsorted(jnp.cumsum(lengths), jnp.arange(rows * top), side="right").astype(jnp.int32)
    table = members.reshape(top, rows).T
    table = table[jax.random.permutation(jax.random.fold_in(own, 1), rows)]
    rotation = jax.random.randint(jax.random.fold_in(own, 2), (rows, 1), 0, top)
    return jnp.take_along_axis(table, (jnp.arange(top)[None, :] + rotation) % top, axis=1)


def portions_of(number_of, total, limit, slope, full):
    portions = [(1 << 20) // math.isqrt(rank ** slope) + 1 for rank in range(1, number_of + 1)]
    largest = limit if full else min(limit, max(-(-total // number_of), total * portions[0] // sum(portions)))
    least = 1 if total - largest >= number_of - 1 else 0
    holding, surplus = [largest] + [least] * (number_of - 1), total - largest - least * (number_of - 1)
    while surplus > 0:
        free = [i for i in range(1, number_of) if holding[i] < largest] or [i for i in range(1, number_of) if holding[i] < limit]
        mass, remaining = sum([portions[i] for i in free]), surplus
        for i in free:
            extra = min(limit - holding[i], max(1, remaining * portions[i] // mass), surplus)
            holding[i] = holding[i] + extra
            surplus = surplus - extra
    return np.array(holding)


def centred(key, dims, spread, bound, pieces=(), held_as=jnp.bfloat16):
    loudness = level_of(key, dims, pieces, -0.22, 0.18) if pieces else 1.0
    drawn = jax.random.normal(key, dims, jnp.float32) * spread * loudness
    return jnp.minimum(jnp.maximum(drawn, -bound), bound).astype(held_as)


def setup_inputs(seed: int = 0) -> dict:
    key_of = jax.random.split(jax.random.key(seed), 9)
    density = jnp.clip(0.5 + 1.5 * jax.random.uniform(key_of[0], (NX, NY, NZ), jnp.float32) ** level_of(key_of[0], (NX, NY, NZ), ((0, 4), (1, 2), (2, 4)), -0.2, 0.2), 0.5, 2.0)
    velocity = centred(key_of[1], (3, NX, NY, NZ), 0.3, 3.0, ((1, 4), (2, 2), (3, 4)), jnp.float32)
    pressure = jnp.clip(0.5 + 1.5 * jax.random.uniform(key_of[2], (NX, NY, NZ), jnp.float32) ** level_of(key_of[2], (NX, NY, NZ), ((0, 4), (1, 2), (2, 4)), -0.2, 0.2), 0.5, 2.0)
    fine_density = jnp.clip(jax.random.uniform(key_of[3], (N_GX, N_GY, BOXES, FX, FY * FZ), jnp.float32, -0.2, 0.2) * level_of(key_of[3], (N_GX, N_GY, BOXES, FX, FY * FZ), ((0, 4), (1, 2), (2, 4)), -0.4, 0.0), -0.2, 0.2)
    fine_velocity = centred(key_of[4], (3, N_GX, N_GY, BOXES, FX, FY * FZ), 0.2, 3.0, ((1, 4), (2, 2), (3, 4)), jnp.float32)
    fine_pressure = jnp.clip(jax.random.uniform(key_of[5], (N_GX, N_GY, BOXES, FX, FY * FZ), jnp.float32, -0.2, 0.2) * level_of(key_of[5], (N_GX, N_GY, BOXES, FX, FY * FZ), ((0, 4), (1, 2), (2, 4)), -0.4, 0.0), -0.2, 0.2)
    box_parent_keys = jax.random.split(jax.random.fold_in(key_of[6], 1), N_GX * N_GY * BOXES // BOX_DEV)
    box_parent_turns = jax.random.permutation(jax.random.fold_in(key_of[6], 3), N_GX * N_GY * BOXES // BOX_DEV)
    box_parent = jax.vmap(lambda own, number: shared_out(jax.random.fold_in(key_of[6], 2), own, number, BOX_DEV, N_GZ, 1, CAP, 2))(box_parent_keys, box_parent_turns).reshape((N_GX, N_GY, BOXES, 1))
    box_shift = touch_ends(jax.random.randint(key_of[7], (N_GX, N_GY, BOXES), 0, CZ - FZ // 2 + 1), jax.random.fold_in(key_of[7], 1), 0, (CZ - FZ // 2 + 1) - 1).astype(jnp.int32)
    return dict(density=density, velocity=velocity, pressure=pressure, fine_density=fine_density, fine_velocity=fine_velocity, fine_pressure=fine_pressure, box_parent=box_parent, box_shift=box_shift)


GAMMA = 1.4
DT_COARSE = 0.05
DT_FINE = 0.025

def to_conserved(primitive):
    density = primitive[0]
    speed_x = primitive[1]
    speed_y = primitive[2]
    speed_z = primitive[3]
    energy = primitive[4] / (GAMMA - 1.0) + 0.5 * density * (speed_x * speed_x + speed_y * speed_y + speed_z * speed_z)
    return jnp.stack([density, density * speed_x, density * speed_y, density * speed_z, energy])

def to_primitive(conserved):
    density = conserved[0]
    speed_x = conserved[1] / density
    speed_y = conserved[2] / density
    speed_z = conserved[3] / density
    pressure = (GAMMA - 1.0) * (conserved[4] - 0.5 * (conserved[1] * speed_x + conserved[2] * speed_y + conserved[3] * speed_z))
    return [density, speed_x, speed_y, speed_z, pressure]

def minmod(first, second):
    return 0.5 * (jnp.sign(first) + jnp.sign(second)) * jnp.minimum(jnp.abs(first), jnp.abs(second))

def side_terms(state, normal):
    density, speed_x, speed_y, speed_z, pressure = state
    speeds = [speed_x, speed_y, speed_z]
    normal_speed = speeds[normal]
    energy = pressure / (GAMMA - 1.0) + 0.5 * density * (speed_x * speed_x + speed_y * speed_y + speed_z * speed_z)
    sound = jnp.sqrt(GAMMA * pressure / density)
    conserved = [density, density * speed_x, density * speed_y, density * speed_z, energy]
    fluxes = [item * normal_speed for item in conserved]
    fluxes[1 + normal] = fluxes[1 + normal] + pressure
    fluxes[4] = fluxes[4] + pressure * normal_speed
    return (speeds, normal_speed, energy, sound, conserved, fluxes)

def star_state(state, speeds, normal_speed, energy, wave, contact, normal):
    density = state[0]
    pressure = state[4]
    factor = density * (wave - normal_speed) / (wave - contact)
    parts = [factor]
    for index in range(3):
        parts.append(factor * (contact if index == normal else speeds[index]))
    parts.append(factor * (energy / density + (contact - normal_speed) * (contact + pressure / (density * (wave - normal_speed)))))
    return parts

def hllc_flux(left, right, normal):
    left_speeds, left_normal, left_energy, left_sound, left_state, left_flux = side_terms(left, normal)
    right_speeds, right_normal, right_energy, right_sound, right_state, right_flux = side_terms(right, normal)
    wave_left = jnp.minimum(left_normal - left_sound, right_normal - right_sound)
    wave_right = jnp.maximum(left_normal + left_sound, right_normal + right_sound)
    mass_left = left[0] * (wave_left - left_normal)
    mass_right = right[0] * (wave_right - right_normal)
    contact = (right[4] - left[4] + mass_left * left_normal - mass_right * right_normal) / (mass_left - mass_right)
    star_left = star_state(left, left_speeds, left_normal, left_energy, wave_left, contact, normal)
    star_right = star_state(right, right_speeds, right_normal, right_energy, wave_right, contact, normal)
    result = []
    for index in range(5):
        flux_starl = left_flux[index] + wave_left * (star_left[index] - left_state[index])
        flux_starr = right_flux[index] + wave_right * (star_right[index] - right_state[index])
        value = jnp.where(wave_left >= 0.0, left_flux[index], jnp.where(contact >= 0.0, flux_starl, jnp.where(wave_right >= 0.0, flux_starr, right_flux[index])))
        result.append(value)
    return result

def face_flux(fields, axis, spacing):
    length = fields[0].shape[axis] - 4
    left = []
    right = []
    for field in fields:
        jumps = lax.slice_in_dim(field, 1, length + 4, axis=axis) - lax.slice_in_dim(field, 0, length + 3, axis=axis)
        slopes = minmod(lax.slice_in_dim(jumps, 0, length + 2, axis=axis), lax.slice_in_dim(jumps, 1, length + 3, axis=axis))
        left.append(lax.slice_in_dim(field, 1, length + 2, axis=axis) + 0.5 * lax.slice_in_dim(slopes, 0, length + 1, axis=axis))
        right.append(lax.slice_in_dim(field, 2, length + 3, axis=axis) - 0.5 * lax.slice_in_dim(slopes, 1, length + 2, axis=axis))
    fluxes = hllc_flux(left, right, axis)
    return [(lax.slice_in_dim(flux, 1, length + 1, axis=axis) - lax.slice_in_dim(flux, 0, length, axis=axis)) / spacing for flux in fluxes]

def tendency(padded, spacing):
    fields = to_primitive(padded)
    extent = padded.shape[1:]
    result = None
    for axis in range(3):
        trimmed = []
        for field in fields:
            for other in range(3):
                if other != axis:
                    field = lax.slice_in_dim(field, 2, extent[other] - 2, axis=other)
            trimmed.append(field)
        change = face_flux(trimmed, axis, spacing)
        if result is None:
            result = [-part for part in change]
        else:
            result = [prior - part for prior, part in zip(result, change)]
    return jnp.stack(result)

def inject_fine(window):
    return jnp.repeat(jnp.repeat(jnp.repeat(window, 2, axis=1), 2, axis=2), 2, axis=3)

def fine_substep(state, ghosts):

    def rate(inner):
        return tendency(ghosts.at[:, 2:-2, 2:-2, 2:-2].set(inner), 0.5)
    section = state + DT_FINE * rate(state)
    return 0.5 * state + 0.5 * (section + DT_FINE * rate(section))

def fine_box(old_window, new_window, detail):
    padded = inject_fine(old_window)
    padded = padded.at[:, 2:-2, 2:-2, 2:-2].add(detail)
    first_ghosts = to_conserved(padded)
    state = first_ghosts[:, 2:-2, 2:-2, 2:-2]
    state = fine_substep(state, first_ghosts)
    second_ghosts = inject_fine(0.5 * (to_conserved(old_window) + new_window))
    return fine_substep(state, second_ghosts)

def coarsen_box(state):
    fields, width_x, width_y, width_z = state.shape
    blocks = state.reshape(fields, width_x // 2, 2, width_y // 2, 2, width_z // 2, 2)
    return lax.optimization_barrier(jnp.sum(blocks, axis=(2, 4, 6))) * 0.125

def periodic(field):
    return jnp.pad(field, ((0, 0), (2, 2), (2, 2), (2, 2)), mode='wrap')

def reference(density, velocity, pressure, fine_density, fine_velocity, fine_pressure, box_parent, box_shift):
    primitive = jnp.concatenate([density[None], velocity, pressure[None]])
    start = to_conserved(primitive)
    section = start + DT_COARSE * tendency(periodic(start), 1.0)
    updated = 0.5 * start + 0.5 * (section + DT_COARSE * tendency(periodic(section), 1.0))
    span = FZ // 2
    owners = N_GX * N_GY * N_GZ
    merged = FY * FZ

    def one_owner(owner):
        col_x = owner // (N_GY * N_GZ)
        col_y = owner // N_GZ % N_GY
        first = owner % N_GZ * BOX_DEV
        parents = lax.dynamic_slice(box_parent, (col_x, col_y, first, jnp.int32(0)), (1, 1, BOX_DEV, 1)).reshape(BOX_DEV)
        shifts = lax.dynamic_slice(box_shift, (col_x, col_y, first), (1, 1, BOX_DEV)).reshape(BOX_DEV)
        corner = (parents * CZ + shifts).astype(jnp.int32)
        cols = ((col_x * CX - 1 + jnp.arange(CX + 2, dtype=jnp.int32)) % NX).astype(jnp.int32)
        rows = ((col_y * CY - 1 + jnp.arange(CY + 2, dtype=jnp.int32)) % NY).astype(jnp.int32)
        old_column = jnp.take(jnp.take(primitive, cols, axis=1), rows, axis=2)
        new_column = jnp.take(jnp.take(updated, cols, axis=1), rows, axis=2)

        def window_of(column, base):
            heights = ((base - 1 + jnp.arange(span + 2, dtype=jnp.int32)) % NZ).astype(jnp.int32)
            return jnp.take(column, heights, axis=3)
        old_windows = jax.vmap(lambda base: window_of(old_column, base))(corner)
        new_windows = jax.vmap(lambda base: window_of(new_column, base))(corner)
        zero = jnp.int32(0)
        part_density = lax.dynamic_slice(fine_density, (col_x, col_y, first, zero, zero), (1, 1, BOX_DEV, FX, merged)).reshape(1, BOX_DEV, FX, FY, FZ)
        part_velocity = lax.dynamic_slice(fine_velocity, (zero, col_x, col_y, first, zero, zero), (3, 1, 1, BOX_DEV, FX, merged)).reshape(3, BOX_DEV, FX, FY, FZ)
        part_pressure = lax.dynamic_slice(fine_pressure, (col_x, col_y, first, zero, zero), (1, 1, BOX_DEV, FX, merged)).reshape(1, BOX_DEV, FX, FY, FZ)
        details = jnp.moveaxis(jnp.concatenate([part_density, part_velocity, part_pressure]), 1, 0)
        finals = jax.vmap(fine_box)(old_windows, new_windows, details)
        means = jax.vmap(coarsen_box)(finals)
        return (finals, means, corner)
    finals, means, corners = lax.map(one_owner, jnp.arange(owners, dtype=jnp.int32))
    fine_state = jnp.moveaxis(finals, 2, 0).reshape(5, N_GX, N_GY, N_GZ * BOX_DEV, FX, merged)
    owner_ids = jnp.arange(owners, dtype=jnp.int32)
    owner_x = owner_ids // (N_GY * N_GZ)
    owner_y = owner_ids // N_GZ % N_GY
    index_x = owner_x[:, None, None, None, None] * CX + jnp.arange(CX, dtype=jnp.int32)[None, None, :, None, None]
    index_y = owner_y[:, None, None, None, None] * CY + jnp.arange(CY, dtype=jnp.int32)[None, None, None, :, None]
    index_z = corners[:, :, None, None, None] + jnp.arange(span, dtype=jnp.int32)[None, None, None, None, :]
    shape_all = (owners, BOX_DEV, CX, CY, span)
    index_x = jnp.broadcast_to(index_x, shape_all).astype(jnp.int32)
    index_y = jnp.broadcast_to(index_y, shape_all).astype(jnp.int32)
    index_z = jnp.broadcast_to(index_z, shape_all).astype(jnp.int32)
    summed = jnp.zeros((5, NX, NY, NZ), jnp.float32).at[:, index_x, index_y, index_z].add(jnp.moveaxis(means, 2, 0))
    count = jnp.zeros((NX, NY, NZ), jnp.float32).at[index_x, index_y, index_z].add(1.0)
    coarse_state = jnp.where(count > 0.0, summed / jnp.maximum(count, 1.0), updated)
    return (coarse_state, fine_state)
```

```python
import functools

import jax
import jax.numpy as jnp
from jax import lax
from jax.experimental import pallas as pl
from jax.experimental.pallas import tpu as pltpu
from jax.sharding import PartitionSpec as P

GAMMA = 1.4
DT_COARSE = 0.05
DT_FINE = 0.025
MESH = pl.DeviceIdType.MESH
F32 = jnp.float32


def mm(a, b):
    return lax.dot_general(
        a,
        b,
        (((1,), (0,)), ((), ())),
        precision=lax.Precision.HIGHEST,
        preferred_element_type=F32,
    )


def to_conserved(q):
    rho, u, v, w, p = q
    energy = p * (1.0 / (GAMMA - 1.0)) + 0.5 * rho * (u * u + v * v + w * w)
    return [rho, rho * u, rho * v, rho * w, energy]


def to_primitive(c):
    rho, mx, my, mz, energy = c
    inv = 1.0 / rho
    u, v, w = mx * inv, my * inv, mz * inv
    p = (GAMMA - 1.0) * (energy - 0.5 * (mx * u + my * v + mz * w))
    return [rho, u, v, w, p]


def minmod(a, b):
    return jnp.maximum(jnp.minimum(a, b), 0.0) + jnp.minimum(jnp.maximum(a, b), 0.0)


def hllc(left, right):
    rl, ul, _, _, pl_ = left
    rr, ur, _, _, pr = right
    cl = jnp.sqrt(GAMMA * pl_ / rl)
    cr = jnp.sqrt(GAMMA * pr / rr)
    sl = jnp.minimum(ul - cl, ur - cr)
    sr = jnp.maximum(ul + cl, ur + cr)
    ml = rl * (sl - ul)
    mr = rr * (sr - ur)
    contact = (pr - pl_ + ml * ul - mr * ur) / (ml - mr)
    use_left = (sl >= 0.0) | (contact >= 0.0)
    rho, un, t1, t2, p = [jnp.where(use_left, a, b) for a, b in zip(left, right)]
    wave = jnp.where(use_left, sl, sr)
    mass = jnp.where(use_left, ml, mr)
    outside = (sl >= 0.0) | (jnp.logical_not(use_left) & (sr < 0.0))
    scale = 1.0 / (wave - contact)
    energy = p * (1.0 / (GAMMA - 1.0)) + 0.5 * rho * (un * un + t1 * t1 + t2 * t2)
    star_rho = mass * scale
    star_energy = ((wave - un) * energy + (contact - un) * (mass * contact + p)) * scale
    flow = rho * un
    zero = jnp.zeros_like(rho)
    f0 = flow + jnp.where(outside, zero, wave * (star_rho - rho))
    fn = flow * un + p + jnp.where(outside, zero, wave * (star_rho * contact - flow))
    fe = (energy + p) * un + jnp.where(outside, zero, wave * (star_energy - energy))
    return [f0, fn, t1 * f0, t2 * f0, fe]


TURN = ((0, 1, 2, 3, 4), (0, 2, 3, 1, 4), (0, 3, 1, 2, 4))


def stacked_flux(lefts, rights):
    sizes = [part[0].shape[0] for _, part in lefts]

    def joined(parts):
        return [jnp.concatenate([part[TURN[axis][i]] for axis, part in parts]) for i in range(5)]

    fluxes = hllc(joined(lefts), joined(rights))
    out = []
    at = 0
    for (axis, _), size in zip(lefts, sizes):
        part = [None] * 5
        for i in range(5):
            part[TURN[axis][i]] = fluxes[i][at : at + size]
        out.append(part)
        at += size
    return out


def roll(a, shift, axis):
    size = a.shape[axis]
    shift = shift % size
    return a if shift == 0 else pltpu.roll(a, shift, axis)


def coarse_tendency(q, n):
    lane = lax.broadcasted_iota(jnp.int32, (1, 8, 128), 2)
    row = lax.broadcasted_iota(jnp.int32, (1, 8, 128), 1)
    inner = (row >= 2) & (row < 6)
    ly, ry, lx, rx, lz, rz = [], [], [], [], [], []
    for f in range(5):
        a = q[f]
        jump = a[1:8] - a[0:7]
        half = 0.5 * minmod(jump[0:6], jump[1:7])
        ly.append(a[1:6] + half[0:5])
        ry.append(a[2:7] - half[1:6])
        c = a[2:6]
        jump = c - roll(c, 1, 1)
        half = 0.5 * minmod(jump, roll(jump, -1, 1))
        lx.append(roll(c + half, 1, 1))
        rx.append(c - half)
        g = n[f]
        before = roll(jnp.where(lane == 127, g, c), 1, 2)
        after = roll(jnp.where(lane == 0, g, c), -1, 2)
        half = 0.5 * minmod(c - before, after - c)
        g_before = roll(jnp.where(lane == 127, c, g), 1, 2)
        g_after = roll(jnp.where(lane == 0, c, g), -1, 2)
        g_half = 0.5 * minmod(g - g_before, g_after - g)
        up = c + half
        down = c - half
        low_left = roll(jnp.where(lane == 127, g + g_half, up), 1, 2)
        high_right = roll(jnp.where(lane == 0, g - g_half, down), -1, 2)
        lz.append(jnp.where(inner, low_left, roll(up, 4, 1)))
        rz.append(jnp.where(inner, down, roll(high_right, 4, 1)))
    fx, fy, fz = stacked_flux([(0, lx), (1, ly), (2, lz)], [(0, rx), (1, ry), (2, rz)])
    out = []
    for f in range(5):
        dx = roll(fx[f], -1, 1) - fx[f]
        dy = fy[f][1:5] - fy[f][0:4]
        dz = roll(fz[f], 4, 1) - fz[f]
        out.append(-dx - dy - dz)
    return out


def fine_tendency(q, ghosts):
    lane = lax.broadcasted_iota(jnp.int32, (1, 8, 128), 2)
    row = lax.broadcasted_iota(jnp.int32, (1, 8, 128), 1)
    firsts = (row == 0, lane < 16, lane % 16 == 0)
    lasts = (row == 7, lane >= 112, lane % 16 == 15)
    steps = ((1, 1), (16, 2), (1, 2))
    lefts, rights, end_lefts, end_rights = [], [], [], []
    for axis in range(3):
        step, dim = steps[axis]
        left, right, tops = [], [], []
        for f in range(5):
            a = q[f]
            g = ghosts[axis][f]
            before = jnp.where(firsts[axis], g, roll(a, step, dim))
            after = jnp.where(lasts[axis], g, roll(a, -step, dim))
            half = 0.5 * minmod(a - before, after - a)
            up = a + half
            left.append(jnp.where(firsts[axis], g, roll(up, step, dim)))
            right.append(a - half)
            tops.append(up)
        lefts.append((axis, left))
        rights.append((axis, right))
        end_lefts.append((axis, tops))
        end_rights.append((axis, ghosts[axis]))
    parts = stacked_flux(lefts + end_lefts, rights + end_rights)
    out = [None] * 5
    for axis in range(3):
        step, dim = steps[axis]
        for f in range(5):
            low = parts[axis][f]
            change = jnp.where(lasts[axis], parts[3 + axis][f], roll(low, -step, dim)) - low
            out[f] = -change if out[f] is None else out[f] - change
    return [2.0 * part for part in out]


def kernel(
    sizes,
    density,
    velocity,
    pressure,
    fine_density,
    fine_velocity,
    fine_pressure,
    parents,
    shifts,
    coarse_out,
    fine_out,
    ext,
    xs,
    xr,
    ys,
    yr,
    zs,
    zr,
    xs1,
    xr1,
    ys1,
    yr1,
    yf,
    sel,
    expand_t,
    expand_y,
    place,
    msg,
    got,
    mean,
    mean_got,
    laid,
    upd,
    send_sem,
    recv_sem,
):
    nx, ny, nz = sizes
    cz = 128
    gx, gy, gz = lax.axis_index("gx"), lax.axis_index("gy"), lax.axis_index("gz")
    x_up, x_dn = {"gx": lax.rem(gx + 1, nx)}, {"gx": lax.rem(gx + nx - 1, nx)}
    y_up, y_dn = {"gy": lax.rem(gy + 1, ny)}, {"gy": lax.rem(gy + ny - 1, ny)}
    column = [lax.rem(gz + d, nz) for d in range(nz)]
    z_up, z_dn = {"gz": column[1]}, {"gz": column[nz - 1]}
    started = []

    def send(src, dst, device):
        at = len(started)
        copy = pltpu.make_async_remote_copy(
            src_ref=src,
            dst_ref=dst,
            send_sem=send_sem.at[at],
            recv_sem=recv_sem.at[at],
            device_id=device,
            device_id_type=MESH,
        )
        copy.start()
        started.append(copy)
        return copy

    barrier = pltpu.get_barrier_semaphore()
    partners = [x_up, x_dn, y_up, y_dn] + [{"gz": column[d]} for d in range(1, nz)]
    for device in partners:
        pl.semaphore_signal(barrier, inc=1, device_id=device, device_id_type=MESH)

    lane1 = lax.broadcasted_iota(jnp.int32, (8, 128), 1)
    lane3 = lax.broadcasted_iota(jnp.int32, (1, 8, 128), 2)

    def pack_z(fields, at):
        packed = jnp.zeros((4, 8, 128), F32)
        for f in range(5):
            packed = jnp.where(lane3 // 4 == f, roll(fields[f], 2 + 4 * f, 2), packed)
        zs[at] = packed

    def start_halos(at):
        for f in range(5):
            xs[at, 0, f] = ext[f, 2:6, 2:4, :]
            xs[at, 1, f] = ext[f, 2:6, 4:6, :]
            ys[at, 0, f] = ext[f, 2:4, 2:6, :]
            ys[at, 1, f] = ext[f, 4:6, 2:6, :]
        if at == 0:
            pl.semaphore_wait(barrier, len(partners))
        return [
            send(xs.at[at, 1], xr.at[at, 0], x_up),
            send(xs.at[at, 0], xr.at[at, 1], x_dn),
            send(ys.at[at, 1], yr.at[at, 0], y_up),
            send(ys.at[at, 0], yr.at[at, 1], y_dn),
            send(zs.at[at], zr.at[at, 0], z_up),
            send(zs.at[at], zr.at[at, 1], z_dn),
        ]

    def take_halos(at, copies):
        for copy in copies:
            copy.wait_recv()
        for f in range(5):
            ext[f, 2:6, 0:2, :] = xr[at, 0, f]
            ext[f, 2:6, 6:8, :] = xr[at, 1, f]
            ext[f, 0:2, 2:6, :] = yr[at, 0, f]
            ext[f, 6:8, 2:6, :] = yr[at, 1, f]
        ends = jnp.where(lane3 % 4 < 2, zr[at, 0], zr[at, 1])
        return [roll(ends, 126 - 4 * f, 2) for f in range(5)]

    def start_windows(at):
        for f in range(5):
            yf[f, 0:4, :] = ext[f, 1, 2:6, :]
            yf[f, 4:8, :] = ext[f, 6, 2:6, :]
        copies = []
        for chunk in range((nz + 3) // 4):
            picked = []
            for r in range(4):
                rows = [ext[f, 2 + r] for f in range(5)] + [yf[r]]
                if r == 0:
                    rows.append(yf[4])
                picked.append(mm(jnp.concatenate(rows), sel[chunk, r]))
            for d in range(4 * chunk, min(4 * chunk + 4, nz)):
                body = jnp.zeros((48, 128), F32)
                group = lax.broadcasted_iota(jnp.int32, (48, 128), 1) // 32
                for r in range(4):
                    body = jnp.where(group == (d + r) % 4, picked[r][0:48], body)
                tail = jnp.where(lane1 // 32 == d % 4, picked[0][48:56], 0.0)
                if d == 0:
                    got[at, 0, 0:48, :] = body
                    got[at, 0, 48:56, :] = tail
                else:
                    msg[at, d - 1, 0:48, :] = body
                    msg[at, d - 1, 48:56, :] = tail
                    copies.append(send(msg.at[at, d - 1], got.at[at, d], {"gz": column[d]}))
        return copies

    def take_windows(at, copies):
        for copy in copies:
            copy.wait_recv()
        total = got[at, 0]
        for d in range(1, nz):
            total = total + roll(got[at, d], -32 * (d % 4), 1)
        inner = [total[8 * f : 8 * f + 8] for f in range(5)]
        faces = [roll(total[40:48], -32 * f, 1) for f in range(4)] + [total[48:56]]
        return inner, faces

    row2 = lax.broadcasted_iota(jnp.int32, (8, 128), 0)

    def doubled(tile, base):
        out = tile[base : base + 1]
        for k in range(1, 4):
            out = jnp.where(row2 >= 2 * k, tile[base + k : base + k + 1], out)
        return jnp.broadcast_to(out, (8, 128))

    def injected(inner, faces):
        rows = [doubled(tile, 2) for tile in inner] + list(inner)
        wide = mm(jnp.concatenate(rows), expand_t[...])
        rows = [doubled(tile, 0) for tile in faces] + [doubled(tile, 4) for tile in faces]
        sides = mm(jnp.concatenate(rows), expand_y[...])

        def both(matrix, first_row, left, right):
            return jnp.stack(
                [
                    matrix[first_row : first_row + 8, left : left + 128],
                    matrix[first_row : first_row + 8, right : right + 128],
                ]
            )

        row = lax.broadcasted_iota(jnp.int32, (1, 8, 128), 1)
        cells, in_x, in_y, in_z = [], [], [], []
        for f in range(5):
            cells.append(both(wide, 8 * f, 0, 128))
            in_z.append(both(wide, 8 * f, 256, 384))
            edge = both(wide, 40 + 8 * f, 0, 128)
            in_x.append(jnp.where(row < 4, edge[:, 1:2, :], edge[:, 6:7, :]))
            low = both(sides, 8 * f, 0, 128)
            high = both(sides, 40 + 8 * f, 0, 128)
            in_y.append(jnp.where(lane3 < 64, low, high))
        return cells, (in_x, in_y, in_z)

    ext[...] = jnp.ones(ext.shape, F32)
    for y in range(4):
        ext[0, 2 + y, 2:6, :] = density[:, y, :]
        for k in range(3):
            ext[1 + k, 2 + y, 2:6, :] = velocity[k, :, y, :]
        ext[4, 2 + y, 2:6, :] = pressure[:, y, :]
    pack_z([ext[f, 2:6] for f in range(5)], 0)
    halos = start_halos(0)

    big_row = lax.broadcasted_iota(jnp.int32, (128, 128), 0)

    def one_hot(index):
        return jnp.where(big_row == index[0:1, :], 1.0, 0.0)

    slot = lane1 % 16
    for chunk in range((nz + 3) // 4):
        target = jnp.full((8, 128), -4 * cz * nz, jnp.int32)
        for d in range(4 * chunk, min(4 * chunk + 4, nz)):
            for b in range(2):
                box = 2 * column[d] + b
                low = parents[box] * cz + shifts[box] - 1
                target = jnp.where(lane1 // 16 == 2 * (d % 4) + b, low + slot, target)
        target = jnp.where(target == -1, target + nz * cz, target)
        target = jnp.where(target >= nz * cz, target - nz * cz, target)
        target = jnp.where(slot < 10, target - gz * cz, -1)
        for r in range(4):
            sel[chunk, r] = one_hot(roll(target, 32 * r, 1))
    fine_y, fine_z = lane1 // 16, lane1 % 16
    for b in range(2):
        base = (fine_y // 2) * 32 + 16 * b
        expand_t[:, 128 * b : 128 * b + 128] = one_hot(base + fine_z // 2 + 1)
        expand_t[:, 256 + 128 * b : 384 + 128 * b] = one_hot(base + jnp.where(fine_z < 8, 0, 9))
        expand_y[:, 128 * b : 128 * b + 128] = one_hot(16 * b + fine_z // 2 + 1)
    big_lane = lax.broadcasted_iota(jnp.int32, (128, 128), 1)
    for pair in range((nz + 1) // 2):
        target = jnp.full((128, 128), -4 * cz, jnp.int32)
        for k in range(2):
            d = 2 * pair + k
            if d < nz:
                owner = column[(nz - d) % nz]
                for b in range(2):
                    box = 2 * owner + b
                    low = jnp.where(parents[box] == gz, shifts[box], -4 * cz)
                    target = jnp.where(big_row // 32 == 2 * k + b, low, target)
        hit = big_lane == target + big_row % 8
        for y in range(4):
            place[pair, :, 128 * y : 128 * y + 128] = jnp.where(
                hit & ((big_row % 32) // 8 == y), 1.0, 0.0
            )
    count = jnp.zeros((8, 128), F32)
    for box in range(2 * nz):
        low = jnp.where(parents[box] == gz, shifts[box], -4 * cz)
        count = count + jnp.where((lane1 >= low) & (lane1 < low + 8), 1.0, 0.0)
    count = count[0:4]

    ends = take_halos(0, halos)
    rim = [ext[f] for f in range(5)]
    change = coarse_tendency(rim, ends)
    start = to_conserved([a[2:6] for a in rim])
    section = [a + DT_COARSE * b for a, b in zip(start, change)]
    section = to_primitive(section)
    windows = start_windows(0)
    for f in range(5):
        ext[f, 2:6, 2:6, :] = section[f][:, 2:6, :]
    pack_z(section, 1)
    halos = start_halos(1)

    ends = take_halos(1, halos)
    rim = [ext[f] for f in range(5)]
    change = coarse_tendency(rim, ends)
    section = to_conserved([a[2:6] for a in rim])
    for f in range(5):
        new = 0.5 * start[f] + 0.5 * (section[f] + DT_COARSE * change[f])
        upd[f] = new
        ext[f, 2:6, 2:6, :] = new[:, 2:6, :]
        xs1[0, f] = new[:, 2:3, :]
        xs1[1, f] = new[:, 5:6, :]
        ys1[0, f] = new[0, 2:6, :]
        ys1[1, f] = new[3, 2:6, :]
    faces_sent = [
        send(xs1.at[1], xr1.at[0], x_up),
        send(xs1.at[0], xr1.at[1], x_dn),
        send(ys1.at[1], yr1.at[0], y_up),
        send(ys1.at[0], yr1.at[1], y_dn),
    ]

    old_inner, old_faces = take_windows(0, windows)
    cells, ghosts = injected(old_inner, old_faces)
    detail = [fine_density[...]] + [fine_velocity[k] for k in range(3)] + [fine_pressure[...]]
    prim = [a + b for a, b in zip(cells, detail)]
    state = to_conserved(prim)
    rate = fine_tendency(prim, ghosts)
    stage = [a + DT_FINE * b for a, b in zip(state, rate)]

    for copy in faces_sent:
        copy.wait_recv()
    for f in range(5):
        ext[f, 2:6, 1:2, :] = xr1[0, f]
        ext[f, 2:6, 6:7, :] = xr1[1, f]
        ext[f, 1, 2:6, :] = yr1[0, f]
        ext[f, 6, 2:6, :] = yr1[1, f]
    windows = start_windows(1)

    rate = fine_tendency(to_primitive(stage), ghosts)
    state = [0.5 * a + 0.5 * (b + DT_FINE * c) for a, b, c in zip(state, stage, rate)]

    new_inner, new_faces = take_windows(1, windows)

    def middle(old, new):
        mixed = [0.5 * (a + b) for a, b in zip(to_conserved(old), new)]
        mixed[0] = jnp.where(mixed[0] == 0.0, 1.0, mixed[0])
        return to_primitive(mixed)

    _, ghosts = injected(middle(old_inner, new_inner), middle(old_faces, new_faces))
    rate = fine_tendency(to_primitive(state), ghosts)
    stage = [a + DT_FINE * b for a, b in zip(state, rate)]
    rate = fine_tendency(to_primitive(stage), ghosts)
    state = [0.5 * a + 0.5 * (b + DT_FINE * c) for a, b, c in zip(state, stage, rate)]

    child = big_row // 32 * 8 + (big_row % 16) // 2
    flat = []
    for b in range(2):
        flat.append(mm(jnp.concatenate([a[b] for a in state]), jnp.where(big_lane == child + 32 * b, 0.125, 0.0)))
    summed = flat[0] + flat[1]
    summed = summed + roll(summed, -1, 0)
    mean[...] = summed
    mean_got[0] = summed
    copies = [send(mean, mean_got.at[d], {"gz": column[d]}) for d in range(1, nz)]
    for f in range(5):
        fine_out[f] = state[f]
    for copy in copies:
        copy.wait_recv()
    total = None
    for pair in range((nz + 1) // 2):
        both = mean_got[2 * pair]
        if 2 * pair + 1 < nz:
            both = both + roll(mean_got[2 * pair + 1], 64, 1)
        part = mm(both, place[pair])
        total = part if total is None else total + part
    for f in range(5):
        for y in range(4):
            laid[f, y] = total[8 * f : 8 * f + 8, 128 * y : 128 * y + 128]
    for f in range(5):
        for y in range(4):
            value = laid[f, y, pl.ds(0, 4, stride=2), :] / jnp.maximum(count, 1.0)
            coarse_out[f, :, y, :] = jnp.where(count > 0.0, value, upd[f, y, 2:6, :])
    for copy in started:
        copy.wait_send()


def on_device(sizes, density, velocity, pressure, fine_density, fine_velocity, fine_pressure, parent, shift):
    nz = sizes[2]
    fine = fine_density.shape[2:]
    vmem = pl.BlockSpec(memory_space=pltpu.VMEM)
    smem = pl.BlockSpec(memory_space=pltpu.SMEM)
    copies = 16 + 3 * (nz - 1)
    chunks = (nz + 3) // 4
    scratch = [
        (5, 8, 8, 128),
        (2, 2, 5, 4, 2, 128),
        (2, 2, 5, 4, 2, 128),
        (2, 2, 5, 2, 4, 128),
        (2, 2, 5, 2, 4, 128),
        (2, 4, 8, 128),
        (2, 2, 4, 8, 128),
        (2, 5, 4, 1, 128),
        (2, 5, 4, 1, 128),
        (2, 5, 4, 128),
        (2, 5, 4, 128),
        (5, 8, 128),
        (chunks, 4, 128, 128),
        (128, 512),
        (128, 256),
        ((nz + 1) // 2, 128, 512),
        (2, nz - 1, 56, 128),
        (2, nz, 56, 128),
        (40, 128),
        (nz, 40, 128),
        (5, 4, 8, 128),
        (5, 4, 8, 128),
    ]
    coarse, fine_state = pl.pallas_call(
        functools.partial(kernel, sizes),
        out_shape=(
            jax.ShapeDtypeStruct((5,) + density.shape, F32),
            jax.ShapeDtypeStruct((5,) + fine, F32),
        ),
        in_specs=[vmem] * 6 + [smem] * 2,
        out_specs=(vmem, vmem),
        scratch_shapes=[pltpu.VMEM(shape, F32) for shape in scratch]
        + [pltpu.SemaphoreType.DMA((copies,)), pltpu.SemaphoreType.DMA((copies,))],
        compiler_params=pltpu.CompilerParams(
            collective_id=0, has_side_effects=True, vmem_limit_bytes=32 * 1024 * 1024
        ),
    )(
        density,
        velocity,
        pressure,
        fine_density.reshape(fine),
        fine_velocity.reshape((3,) + fine),
        fine_pressure.reshape(fine),
        parent.reshape(-1),
        shift.reshape(-1),
    )
    return coarse, fine_state.reshape((5, 1, 1) + fine)


def solution(mesh):
    sizes = tuple(mesh.shape[axis] for axis in ("gx", "gy", "gz"))
    in_specs = (
        P("gx", "gy", "gz"),
        P(None, "gx", "gy", "gz"),
        P("gx", "gy", "gz"),
        P("gx", "gy", "gz", None, None),
        P(None, "gx", "gy", "gz", None, None),
        P("gx", "gy", "gz", None, None),
        P("gx", "gy", None, None),
        P("gx", "gy", None),
    )
    out_specs = (P(None, "gx", "gy", "gz"), P(None, "gx", "gy", "gz", None, None))
    return jax.shard_map(
        functools.partial(on_device, sizes),
        mesh=mesh,
        in_specs=in_specs,
        out_specs=out_specs,
        check_vma=False,
    )
```

```python
import functools

import jax
import jax.numpy as jnp
from jax import lax
from jax.experimental import pallas as pl
from jax.experimental.pallas import tpu as pltpu
from jax.sharding import PartitionSpec as P

GAMMA = 1.4
DT_COARSE = 0.05
DT_FINE = 0.025
MESH = pl.DeviceIdType.MESH
F32 = jnp.float32
BF16 = jnp.bfloat16


def mm(a, b):
    size = a.shape[0]
    high = a.astype(BF16).astype(F32)
    rest = a - high
    middle = rest.astype(BF16).astype(F32)
    parts = jnp.concatenate([high, middle, rest - middle]).astype(BF16)
    out = lax.dot_general(parts, b, (((1,), (0,)), ((), ())), preferred_element_type=F32)
    return (out[0:size] + out[size : 2 * size]) + out[2 * size : 3 * size]


def to_conserved(q):
    rho, u, v, w, p = q
    energy = p * (1.0 / (GAMMA - 1.0)) + 0.5 * rho * (u * u + v * v + w * w)
    return [rho, rho * u, rho * v, rho * w, energy]


def to_primitive(c):
    rho, mx, my, mz, energy = c
    inv = 1.0 / rho
    u, v, w = mx * inv, my * inv, mz * inv
    p = (GAMMA - 1.0) * (energy - 0.5 * (mx * u + my * v + mz * w))
    return [rho, u, v, w, p]


def minmod(a, b):
    return jnp.maximum(jnp.minimum(a, b), 0.0) + jnp.minimum(jnp.maximum(a, b), 0.0)


def hllc(left, right):
    rl, ul, _, _, pl_ = left
    rr, ur, _, _, pr = right
    cl = jnp.sqrt(GAMMA * pl_ / rl)
    cr = jnp.sqrt(GAMMA * pr / rr)
    sl = jnp.minimum(ul - cl, ur - cr)
    sr = jnp.maximum(ul + cl, ur + cr)
    ml = rl * (sl - ul)
    mr = rr * (sr - ur)
    contact = (pr - pl_ + ml * ul - mr * ur) / (ml - mr)
    use_left = (sl >= 0.0) | (contact >= 0.0)
    rho, un, t1, t2, p = [jnp.where(use_left, a, b) for a, b in zip(left, right)]
    wave = jnp.where(use_left, sl, sr)
    mass = jnp.where(use_left, ml, mr)
    outside = (sl >= 0.0) | (jnp.logical_not(use_left) & (sr < 0.0))
    scale = 1.0 / (wave - contact)
    energy = p * (1.0 / (GAMMA - 1.0)) + 0.5 * rho * (un * un + t1 * t1 + t2 * t2)
    star_rho = mass * scale
    star_energy = ((wave - un) * energy + (contact - un) * (mass * contact + p)) * scale
    flow = rho * un
    zero = jnp.zeros_like(rho)
    f0 = flow + jnp.where(outside, zero, wave * (star_rho - rho))
    fn = flow * un + p + jnp.where(outside, zero, wave * (star_rho * contact - flow))
    fe = (energy + p) * un + jnp.where(outside, zero, wave * (star_energy - energy))
    return [f0, fn, t1 * f0, t2 * f0, fe]


TURN = ((0, 1, 2, 3, 4), (0, 2, 3, 1, 4), (0, 3, 1, 2, 4))


def stacked_flux(lefts, rights):
    sizes = [part[0].shape[0] for _, part in lefts]

    def joined(parts):
        return [jnp.concatenate([part[TURN[axis][i]] for axis, part in parts]) for i in range(5)]

    fluxes = hllc(joined(lefts), joined(rights))
    out = []
    at = 0
    for (axis, _), size in zip(lefts, sizes):
        part = [None] * 5
        for i in range(5):
            part[TURN[axis][i]] = fluxes[i][at : at + size]
        out.append(part)
        at += size
    return out


def roll(a, shift, axis):
    size = a.shape[axis]
    shift = shift % size
    return a if shift == 0 else pltpu.roll(a, shift, axis)


def coarse_tendency(q, n):
    lane = lax.broadcasted_iota(jnp.int32, (1, 8, 128), 2)
    row = lax.broadcasted_iota(jnp.int32, (1, 8, 128), 1)
    inner = (row >= 2) & (row < 6)
    ly, ry, lx, rx, lz, rz = [], [], [], [], [], []
    for f in range(5):
        a = q[f]
        jump = a[1:8] - a[0:7]
        half = 0.5 * minmod(jump[0:6], jump[1:7])
        ly.append(a[1:6] + half[0:5])
        ry.append(a[2:7] - half[1:6])
        c = a[2:6]
        jump = c - roll(c, 1, 1)
        half = 0.5 * minmod(jump, roll(jump, -1, 1))
        lx.append(roll(c + half, 1, 1))
        rx.append(c - half)
        g = n[f]
        before = roll(jnp.where(lane == 127, g, c), 1, 2)
        after = roll(jnp.where(lane == 0, g, c), -1, 2)
        half = 0.5 * minmod(c - before, after - c)
        g_before = roll(jnp.where(lane == 127, c, g), 1, 2)
        g_after = roll(jnp.where(lane == 0, c, g), -1, 2)
        g_half = 0.5 * minmod(g - g_before, g_after - g)
        up = c + half
        down = c - half
        low_left = roll(jnp.where(lane == 127, g + g_half, up), 1, 2)
        high_right = roll(jnp.where(lane == 0, g - g_half, down), -1, 2)
        lz.append(jnp.where(inner, low_left, roll(up, 4, 1)))
        rz.append(jnp.where(inner, down, roll(high_right, 4, 1)))
    fx, fy, fz = stacked_flux([(0, lx), (1, ly), (2, lz)], [(0, rx), (1, ry), (2, rz)])
    out = []
    for f in range(5):
        dx = roll(fx[f], -1, 1) - fx[f]
        dy = fy[f][1:5] - fy[f][0:4]
        dz = roll(fz[f], 4, 1) - fz[f]
        out.append(-dx - dy - dz)
    return out


def fine_tendency(q, ghosts):
    lane = lax.broadcasted_iota(jnp.int32, (1, 8, 128), 2)
    row = lax.broadcasted_iota(jnp.int32, (1, 8, 128), 1)
    firsts = (row == 0, lane < 16, lane % 16 == 0)
    lasts = (row == 7, lane >= 112, lane % 16 == 15)
    steps = ((1, 1), (16, 2), (1, 2))
    lefts, rights, end_lefts, end_rights = [], [], [], []
    for axis in range(3):
        step, dim = steps[axis]
        left, right, tops = [], [], []
        for f in range(5):
            a = q[f]
            g = ghosts[axis][f]
            before = jnp.where(firsts[axis], g, roll(a, step, dim))
            after = jnp.where(lasts[axis], g, roll(a, -step, dim))
            half = 0.5 * minmod(a - before, after - a)
            up = a + half
            left.append(jnp.where(firsts[axis], g, roll(up, step, dim)))
            right.append(a - half)
            tops.append(up)
        lefts.append((axis, left))
        rights.append((axis, right))
        end_lefts.append((axis, tops))
        end_rights.append((axis, ghosts[axis]))
    parts = stacked_flux(lefts + end_lefts, rights + end_rights)
    out = [None] * 5
    for axis in range(3):
        step, dim = steps[axis]
        for f in range(5):
            low = parts[axis][f]
            change = jnp.where(lasts[axis], parts[3 + axis][f], roll(low, -step, dim)) - low
            out[f] = -change if out[f] is None else out[f] - change
    return [2.0 * part for part in out]


def kernel(
    sizes,
    density_in,
    velocity_in,
    pressure_in,
    fine_density_in,
    fine_velocity_in,
    fine_pressure_in,
    parents_in,
    shifts_in,
    coarse_to,
    fine_to,
    coarse_out,
    fine_out,
    density,
    velocity,
    pressure,
    fine_density,
    fine_velocity,
    fine_pressure,
    ext,
    xs,
    xr,
    ys,
    yr,
    zs,
    zr,
    xs1,
    xr1,
    ys1,
    yr1,
    yf,
    msg,
    got,
    mean,
    mean_got,
    laid,
    upd,
    sel,
    expand_t,
    expand_y,
    place,
    parents,
    shifts,
    load_sem,
    send_sem,
    recv_sem,
):
    nx, ny, nz = sizes
    cz = 128
    gx, gy, gz = lax.axis_index("gx"), lax.axis_index("gy"), lax.axis_index("gz")
    x_up, x_dn = {"gx": lax.rem(gx + 1, nx)}, {"gx": lax.rem(gx + nx - 1, nx)}
    y_up, y_dn = {"gy": lax.rem(gy + 1, ny)}, {"gy": lax.rem(gy + ny - 1, ny)}
    column = [lax.rem(gz + d, nz) for d in range(nz)]
    z_up, z_dn = {"gz": column[1]}, {"gz": column[nz - 1]}
    started = []

    def send(src, dst, device):
        at = len(started)
        copy = pltpu.make_async_remote_copy(
            src_ref=src,
            dst_ref=dst,
            send_sem=send_sem.at[at],
            recv_sem=recv_sem.at[at],
            device_id=device,
            device_id_type=MESH,
        )
        copy.start()
        started.append(copy)
        return copy

    loads = []
    for src, dst in (
        (density_in, density),
        (velocity_in, velocity),
        (pressure_in, pressure),
        (parents_in, parents),
        (shifts_in, shifts),
        (fine_density_in, fine_density),
        (fine_velocity_in, fine_velocity),
        (fine_pressure_in, fine_pressure),
    ):
        load = pltpu.make_async_copy(src, dst, load_sem.at[len(loads)])
        load.start()
        loads.append(load)

    barrier = pltpu.get_barrier_semaphore()
    partners = [x_up, x_dn, y_up, y_dn] + [{"gz": column[d]} for d in range(1, nz)]
    for device in partners:
        pl.semaphore_signal(barrier, inc=1, device_id=device, device_id_type=MESH)

    lane1 = lax.broadcasted_iota(jnp.int32, (8, 128), 1)
    lane3 = lax.broadcasted_iota(jnp.int32, (1, 8, 128), 2)

    def pack_z(fields, at):
        packed = jnp.zeros((4, 8, 128), F32)
        for f in range(5):
            packed = jnp.where(lane3 // 4 == f, roll(fields[f], 2 + 4 * f, 2), packed)
        zs[at] = packed

    def start_halos(fields, at):
        pack_z(fields, at)
        for f in range(5):
            xs[at, 0, f] = fields[f][:, 2:4, :]
            xs[at, 1, f] = fields[f][:, 4:6, :]
            ys[at, 0, f] = fields[f][0:2, 2:6, :]
            ys[at, 1, f] = fields[f][2:4, 2:6, :]
        if at == 0:
            pl.semaphore_wait(barrier, len(partners))
        return [
            send(xs.at[at, 1], xr.at[at, 0], x_up),
            send(xs.at[at, 0], xr.at[at, 1], x_dn),
            send(ys.at[at, 1], yr.at[at, 0], y_up),
            send(ys.at[at, 0], yr.at[at, 1], y_dn),
            send(zs.at[at], zr.at[at, 0], z_up),
            send(zs.at[at], zr.at[at, 1], z_dn),
        ]

    def take_halos(at, copies):
        for copy in copies:
            copy.wait_recv()
        for f in range(5):
            ext[f, 2:6, 0:2, :] = xr[at, 0, f]
            ext[f, 2:6, 6:8, :] = xr[at, 1, f]
            ext[f, 0:2, 2:6, :] = yr[at, 0, f]
            ext[f, 6:8, 2:6, :] = yr[at, 1, f]
        ends = jnp.where(lane3 % 4 < 2, zr[at, 0], zr[at, 1])
        return [roll(ends, 126 - 4 * f, 2) for f in range(5)]

    def start_windows(at):
        for f in range(5):
            yf[f, 0:4, :] = ext[f, 1, 2:6, :]
            yf[f, 4:8, :] = ext[f, 6, 2:6, :]
        copies = []
        for chunk in range((nz + 3) // 4):
            picked = []
            for r in range(4):
                rows = [ext[f, 2 + r] for f in range(5)] + [yf[r]]
                if r == 0:
                    rows += [yf[4], yf[4]]
                picked.append(mm(jnp.concatenate(rows), sel[chunk, r]))
            for d in range(4 * chunk, min(4 * chunk + 4, nz)):
                body = jnp.zeros((48, 128), F32)
                group = lax.broadcasted_iota(jnp.int32, (48, 128), 1) // 32
                for r in range(4):
                    body = jnp.where(group == (d + r) % 4, picked[r][0:48], body)
                tail = jnp.where(lane1 // 32 == d % 4, picked[0][48:56], 0.0)
                if d == 0:
                    got[at, 0, 0:48, :] = body
                    got[at, 0, 48:56, :] = tail
                else:
                    msg[at, d - 1, 0:48, :] = body
                    msg[at, d - 1, 48:56, :] = tail
                    copies.append(send(msg.at[at, d - 1], got.at[at, d], {"gz": column[d]}))
        return copies

    def take_windows(at, copies):
        for copy in copies:
            copy.wait_recv()
        total = got[at, 0]
        for d in range(1, nz):
            total = total + roll(got[at, d], -32 * (d % 4), 1)
        inner = [total[8 * f : 8 * f + 8] for f in range(5)]
        faces = [roll(total[40:48], -32 * f, 1) for f in range(4)] + [total[48:56]]
        return inner, faces

    row2 = lax.broadcasted_iota(jnp.int32, (8, 128), 0)

    def doubled(tile, base):
        out = tile[base : base + 1]
        for k in range(1, 4):
            out = jnp.where(row2 >= 2 * k, tile[base + k : base + k + 1], out)
        return jnp.broadcast_to(out, (8, 128))

    def injected(inner, faces):
        rows = [doubled(tile, 2) for tile in inner] + list(inner)
        wide = mm(jnp.concatenate(rows), expand_t[...])
        rows = [doubled(tile, 0) for tile in faces] + [doubled(tile, 4) for tile in faces]
        sides = mm(jnp.concatenate(rows), expand_y[...])

        def both(matrix, first_row, left, right):
            return jnp.stack(
                [
                    matrix[first_row : first_row + 8, left : left + 128],
                    matrix[first_row : first_row + 8, right : right + 128],
                ]
            )

        row = lax.broadcasted_iota(jnp.int32, (1, 8, 128), 1)
        cells, in_x, in_y, in_z = [], [], [], []
        for f in range(5):
            cells.append(both(wide, 8 * f, 0, 128))
            in_z.append(both(wide, 8 * f, 256, 384))
            edge = both(wide, 40 + 8 * f, 0, 128)
            in_x.append(jnp.where(row < 4, edge[:, 1:2, :], edge[:, 6:7, :]))
            low = both(sides, 8 * f, 0, 128)
            high = both(sides, 40 + 8 * f, 0, 128)
            in_y.append(jnp.where(lane3 < 64, low, high))
        return cells, (in_x, in_y, in_z)

    ext[...] = jnp.ones(ext.shape, F32)
    for load in loads[0:3]:
        load.wait()
    for y in range(4):
        ext[0, 2 + y, 2:6, :] = density[:, y, :]
        for k in range(3):
            ext[1 + k, 2 + y, 2:6, :] = velocity[k, :, y, :]
        ext[4, 2 + y, 2:6, :] = pressure[:, y, :]
    halos = start_halos([ext[f, 2:6] for f in range(5)], 0)
    for load in loads[3:8]:
        load.wait()

    big_row = lax.broadcasted_iota(jnp.int32, (128, 128), 0)

    def one_hot(index):
        return jnp.where(big_row == index[0:1, :], 1.0, 0.0).astype(BF16)

    slot = lane1 % 16
    for chunk in range((nz + 3) // 4):
        target = jnp.full((8, 128), -4 * cz * nz, jnp.int32)
        for d in range(4 * chunk, min(4 * chunk + 4, nz)):
            for b in range(2):
                box = 2 * column[d] + b
                low = parents[box] * cz + shifts[box] - 1
                target = jnp.where(lane1 // 16 == 2 * (d % 4) + b, low + slot, target)
        target = jnp.where(target == -1, target + nz * cz, target)
        target = jnp.where(target >= nz * cz, target - nz * cz, target)
        target = jnp.where(slot < 10, target - gz * cz, -1)
        for r in range(4):
            sel[chunk, r] = one_hot(roll(target, 32 * r, 1))
    fine_y, fine_z = lane1 // 16, lane1 % 16
    for b in range(2):
        base = (fine_y // 2) * 32 + 16 * b
        expand_t[:, 128 * b : 128 * b + 128] = one_hot(base + fine_z // 2 + 1)
        expand_t[:, 256 + 128 * b : 384 + 128 * b] = one_hot(base + jnp.where(fine_z < 8, 0, 9))
        expand_y[:, 128 * b : 128 * b + 128] = one_hot(16 * b + fine_z // 2 + 1)
    big_lane = lax.broadcasted_iota(jnp.int32, (128, 128), 1)
    for pair in range((nz + 1) // 2):
        target = jnp.full((128, 128), -4 * cz, jnp.int32)
        for k in range(2):
            d = 2 * pair + k
            if d < nz:
                owner = column[(nz - d) % nz]
                for b in range(2):
                    box = 2 * owner + b
                    low = jnp.where(parents[box] == gz, shifts[box], -4 * cz)
                    target = jnp.where(big_row // 32 == 2 * k + b, low, target)
        hit = big_lane == target + big_row % 8
        for y in range(4):
            place[128 * pair : 128 * pair + 128, 128 * y : 128 * y + 128] = jnp.where(
                hit & ((big_row % 32) // 8 == y), 1.0, 0.0
            ).astype(BF16)
    count = jnp.zeros((8, 128), F32)
    for box in range(2 * nz):
        low = jnp.where(parents[box] == gz, shifts[box], -4 * cz)
        count = count + jnp.where((lane1 >= low) & (lane1 < low + 8), 1.0, 0.0)
    covered = count[0:4] > 0.0
    share = 1.0 / jnp.maximum(count[0:4], 1.0)

    ends = take_halos(0, halos)
    rim = [ext[f] for f in range(5)]
    change = coarse_tendency(rim, ends)
    start = to_conserved([a[2:6] for a in rim])
    section = [a + DT_COARSE * b for a, b in zip(start, change)]
    section = to_primitive(section)
    halos = start_halos(section, 1)
    windows = start_windows(0)
    for f in range(5):
        ext[f, 2:6, 2:6, :] = section[f][:, 2:6, :]

    ends = take_halos(1, halos)
    rim = [ext[f] for f in range(5)]
    change = coarse_tendency(rim, ends)
    section = to_conserved([a[2:6] for a in rim])
    for f in range(5):
        new = 0.5 * start[f] + 0.5 * (section[f] + DT_COARSE * change[f])
        upd[f] = new
        ext[f, 2:6, 2:6, :] = new[:, 2:6, :]
        xs1[0, f] = new[:, 2:3, :]
        xs1[1, f] = new[:, 5:6, :]
        ys1[0, f] = new[0, 2:6, :]
        ys1[1, f] = new[3, 2:6, :]
    faces_sent = [
        send(xs1.at[1], xr1.at[0], x_up),
        send(xs1.at[0], xr1.at[1], x_dn),
        send(ys1.at[1], yr1.at[0], y_up),
        send(ys1.at[0], yr1.at[1], y_dn),
    ]

    old_inner, old_faces = take_windows(0, windows)
    cells, ghosts = injected(old_inner, old_faces)
    detail = [fine_density[...]] + [fine_velocity[k] for k in range(3)] + [fine_pressure[...]]
    prim = [a + b for a, b in zip(cells, detail)]
    state = to_conserved(prim)
    rate = fine_tendency(prim, ghosts)
    stage = [a + DT_FINE * b for a, b in zip(state, rate)]

    for copy in faces_sent:
        copy.wait_recv()
    for f in range(5):
        ext[f, 2:6, 1:2, :] = xr1[0, f]
        ext[f, 2:6, 6:7, :] = xr1[1, f]
        ext[f, 1, 2:6, :] = yr1[0, f]
        ext[f, 6, 2:6, :] = yr1[1, f]
    windows = start_windows(1)

    rate = fine_tendency(to_primitive(stage), ghosts)
    state = [0.5 * a + 0.5 * (b + DT_FINE * c) for a, b, c in zip(state, stage, rate)]

    new_inner, new_faces = take_windows(1, windows)

    def middle(old, new):
        mixed = [0.5 * (a + b) for a, b in zip(to_conserved(old), new)]
        mixed[0] = jnp.where(mixed[0] == 0.0, 1.0, mixed[0])
        return to_primitive(mixed)

    _, ghosts = injected(middle(old_inner, new_inner), middle(old_faces, new_faces))
    rate = fine_tendency(to_primitive(state), ghosts)
    stage = [a + DT_FINE * b for a, b in zip(state, rate)]
    rate = fine_tendency(to_primitive(stage), ghosts)
    state = [0.5 * a + 0.5 * (b + DT_FINE * c) for a, b, c in zip(state, stage, rate)]

    child = big_row // 32 * 8 + (big_row % 16) // 2
    matrix = jnp.where(big_lane == child, 0.125, 0.0).astype(BF16)
    flat = mm(jnp.concatenate([a[b] for b in range(2) for a in state]), matrix)
    summed = flat[0:40] + roll(flat[40:80], 32, 1)
    summed = summed + roll(summed, -1, 0)
    mean[...] = summed
    mean_got[0] = summed
    copies = [send(mean, mean_got.at[d], {"gz": column[d]}) for d in range(1, nz)]
    for f in range(5):
        fine_out[f] = state[f]
    fine_store = pltpu.make_async_copy(fine_out, fine_to, load_sem.at[8])
    fine_store.start()
    for copy in copies:
        copy.wait_recv()
    rows = []
    for pair in range((nz + 1) // 2):
        both = mean_got[2 * pair]
        if 2 * pair + 1 < nz:
            both = both + roll(mean_got[2 * pair + 1], 64, 1)
        rows.append(jnp.concatenate([both, jnp.zeros((8, 128), F32)]))
    total = mm(jnp.concatenate(rows, axis=1), place[...])
    for f in range(5):
        for y in range(4):
            laid[f, y] = total[8 * f : 8 * f + 8, 128 * y : 128 * y + 128]
    for f in range(5):
        for y in range(4):
            value = laid[f, y, pl.ds(0, 4, stride=2), :] * share
            coarse_out[f, :, y, :] = jnp.where(covered, value, upd[f, y, 2:6, :])
    coarse_store = pltpu.make_async_copy(coarse_out, coarse_to, load_sem.at[9])
    coarse_store.start()
    for copy in started:
        copy.wait_send()
    fine_store.wait()
    coarse_store.wait()


def hand_over(coarse, fine, coarse_out, fine_out, sems):
    first = pltpu.make_async_copy(coarse, coarse_out, sems.at[0])
    second = pltpu.make_async_copy(fine, fine_out, sems.at[1])
    first.start()
    second.start()
    first.wait()
    second.wait()


def on_device(sizes, density, velocity, pressure, fine_density, fine_velocity, fine_pressure, parent, shift):
    nz = sizes[2]
    fine = fine_density.shape[2:]
    hbm = pl.BlockSpec(memory_space=pltpu.HBM)
    copies = 16 + 3 * (nz - 1)
    chunks = (nz + 3) // 4
    scratch = [
        (5,) + density.shape,
        (5,) + fine,
        density.shape,
        velocity.shape,
        pressure.shape,
        fine,
        (3,) + fine,
        fine,
        (5, 8, 8, 128),
        (2, 2, 5, 4, 2, 128),
        (2, 2, 5, 4, 2, 128),
        (2, 2, 5, 2, 4, 128),
        (2, 2, 5, 2, 4, 128),
        (2, 4, 8, 128),
        (2, 2, 4, 8, 128),
        (2, 5, 4, 1, 128),
        (2, 5, 4, 1, 128),
        (2, 5, 4, 128),
        (2, 5, 4, 128),
        (5, 8, 128),
        (2, nz - 1, 56, 128),
        (2, nz, 56, 128),
        (40, 128),
        (nz, 40, 128),
        (5, 4, 8, 128),
        (5, 4, 8, 128),
    ]
    matrices = [(chunks, 4, 128, 128), (128, 512), (128, 256), (128 * ((nz + 1) // 2), 512)]
    coarse, fine_state = pl.pallas_call(
        functools.partial(kernel, sizes),
        out_shape=(
            jax.ShapeDtypeStruct((5,) + density.shape, F32),
            jax.ShapeDtypeStruct((5,) + fine, F32),
        ),
        in_specs=[hbm] * 8,
        out_specs=(hbm, hbm),
        scratch_shapes=[pltpu.VMEM(shape, F32) for shape in scratch]
        + [pltpu.VMEM(shape, BF16) for shape in matrices]
        + [pltpu.SMEM((2 * nz,), jnp.int32)] * 2
        + [pltpu.SemaphoreType.DMA((10,)), pltpu.SemaphoreType.DMA((copies,)), pltpu.SemaphoreType.DMA((copies,))],
        compiler_params=pltpu.CompilerParams(
            collective_id=0, has_side_effects=True, vmem_limit_bytes=56 * 1024 * 1024
        ),
    )(
        density,
        velocity,
        pressure,
        fine_density.reshape(fine),
        fine_velocity.reshape((3,) + fine),
        fine_pressure.reshape(fine),
        parent.reshape(-1),
        shift.reshape(-1),
    )
    coarse, fine_state = pl.pallas_call(
        hand_over,
        out_shape=(
            jax.ShapeDtypeStruct(coarse.shape, F32),
            jax.ShapeDtypeStruct(fine_state.shape, F32),
        ),
        in_specs=[hbm, hbm],
        out_specs=(hbm, hbm),
        scratch_shapes=[pltpu.SemaphoreType.DMA((2,))],
        compiler_params=pltpu.CompilerParams(vmem_limit_bytes=56 * 1024 * 1024),
    )(coarse, fine_state)
    return coarse, fine_state.reshape((5, 1, 1) + fine)


def solution(mesh):
    sizes = tuple(mesh.shape[axis] for axis in ("gx", "gy", "gz"))
    in_specs = (
        P("gx", "gy", "gz"),
        P(None, "gx", "gy", "gz"),
        P("gx", "gy", "gz"),
        P("gx", "gy", "gz", None, None),
        P(None, "gx", "gy", "gz", None, None),
        P("gx", "gy", "gz", None, None),
        P("gx", "gy", None, None),
        P("gx", "gy", None),
    )
    out_specs = (P(None, "gx", "gy", "gz"), P(None, "gx", "gy", "gz", None, None))
    return jax.shard_map(
        functools.partial(on_device, sizes),
        mesh=mesh,
        in_specs=in_specs,
        out_specs=out_specs,
        check_vma=False,
    )
```

```python
import functools

import jax
import jax.numpy as jnp
from jax import lax
from jax.experimental import pallas as pl
from jax.experimental.pallas import tpu as pltpu
from jax.sharding import PartitionSpec as P

GAMMA = 1.4
DT_COARSE = 0.05
DT_FINE = 0.025
MESH = pl.DeviceIdType.MESH
F32 = jnp.float32
BF16 = jnp.bfloat16


def mm(a, b):
    size = a.shape[0]
    high = a.astype(BF16).astype(F32)
    rest = a - high
    middle = rest.astype(BF16).astype(F32)
    parts = jnp.concatenate([high, middle, rest - middle]).astype(BF16)
    out = lax.dot_general(parts, b, (((1,), (0,)), ((), ())), preferred_element_type=F32)
    return (out[0:size] + out[size : 2 * size]) + out[2 * size : 3 * size]


def to_conserved(q):
    rho, u, v, w, p = q
    energy = p * (1.0 / (GAMMA - 1.0)) + 0.5 * rho * (u * u + v * v + w * w)
    return [rho, rho * u, rho * v, rho * w, energy]


def to_primitive(c):
    rho, mx, my, mz, energy = c
    inv = 1.0 / rho
    u, v, w = mx * inv, my * inv, mz * inv
    p = (GAMMA - 1.0) * (energy - 0.5 * (mx * u + my * v + mz * w))
    return [rho, u, v, w, p]


def minmod(a, b):
    return jnp.maximum(jnp.minimum(a, b), 0.0) + jnp.minimum(jnp.maximum(a, b), 0.0)


def hllc(left, right):
    rl, ul, _, _, pl_ = left
    rr, ur, _, _, pr = right
    cl = jnp.sqrt(GAMMA * pl_ / rl)
    cr = jnp.sqrt(GAMMA * pr / rr)
    sl = jnp.minimum(ul - cl, ur - cr)
    sr = jnp.maximum(ul + cl, ur + cr)
    ml = rl * (sl - ul)
    mr = rr * (sr - ur)
    contact = (pr - pl_ + ml * ul - mr * ur) / (ml - mr)
    use_left = (sl >= 0.0) | (contact >= 0.0)
    rho, un, t1, t2, p = [jnp.where(use_left, a, b) for a, b in zip(left, right)]
    wave = jnp.where(use_left, sl, sr)
    mass = jnp.where(use_left, ml, mr)
    outside = (sl >= 0.0) | (jnp.logical_not(use_left) & (sr < 0.0))
    scale = 1.0 / (wave - contact)
    energy = p * (1.0 / (GAMMA - 1.0)) + 0.5 * rho * (un * un + t1 * t1 + t2 * t2)
    star_rho = mass * scale
    star_energy = ((wave - un) * energy + (contact - un) * (mass * contact + p)) * scale
    flow = rho * un
    zero = jnp.zeros_like(rho)
    f0 = flow + jnp.where(outside, zero, wave * (star_rho - rho))
    fn = flow * un + p + jnp.where(outside, zero, wave * (star_rho * contact - flow))
    fe = (energy + p) * un + jnp.where(outside, zero, wave * (star_energy - energy))
    return [f0, fn, t1 * f0, t2 * f0, fe]


TURN = ((0, 1, 2, 3, 4), (0, 2, 3, 1, 4), (0, 3, 1, 2, 4))


def stacked_flux(lefts, rights):
    sizes = [part[0].shape[0] for _, part in lefts]

    def joined(parts):
        return [jnp.concatenate([part[TURN[axis][i]] for axis, part in parts]) for i in range(5)]

    fluxes = hllc(joined(lefts), joined(rights))
    out = []
    at = 0
    for (axis, _), size in zip(lefts, sizes):
        part = [None] * 5
        for i in range(5):
            part[TURN[axis][i]] = fluxes[i][at : at + size]
        out.append(part)
        at += size
    return out


def roll(a, shift, axis):
    size = a.shape[axis]
    shift = shift % size
    return a if shift == 0 else pltpu.roll(a, shift, axis)


def coarse_fluxes_yz(q, n):
    lane = lax.broadcasted_iota(jnp.int32, (1, 8, 128), 2)
    row = lax.broadcasted_iota(jnp.int32, (1, 8, 128), 1)
    inner = (row >= 2) & (row < 6)
    ly, ry, lz, rz = [], [], [], []
    for f in range(5):
        a = q[f]
        jump = a[1:8] - a[0:7]
        half = 0.5 * minmod(jump[0:6], jump[1:7])
        ly.append(a[1:6] + half[0:5])
        ry.append(a[2:7] - half[1:6])
        c = a[2:6]
        g = n[f]
        before = roll(jnp.where(lane == 127, g, c), 1, 2)
        after = roll(jnp.where(lane == 0, g, c), -1, 2)
        half = 0.5 * minmod(c - before, after - c)
        g_before = roll(jnp.where(lane == 127, c, g), 1, 2)
        g_after = roll(jnp.where(lane == 0, c, g), -1, 2)
        g_half = 0.5 * minmod(g - g_before, g_after - g)
        up = c + half
        down = c - half
        low_left = roll(jnp.where(lane == 127, g + g_half, up), 1, 2)
        high_right = roll(jnp.where(lane == 0, g - g_half, down), -1, 2)
        lz.append(jnp.where(inner, low_left, roll(up, 4, 1)))
        rz.append(jnp.where(inner, down, roll(high_right, 4, 1)))
    fy, fz = stacked_flux([(1, ly), (2, lz)], [(1, ry), (2, rz)])
    out = []
    for f in range(5):
        dy = fy[f][1:5] - fy[f][0:4]
        dz = roll(fz[f], 4, 1) - fz[f]
        out.append(-dy - dz)
    return out


def coarse_fluxes_x(q):
    lx, rx = [], []
    for c in q:
        jump = c - roll(c, 1, 1)
        half = 0.5 * minmod(jump, roll(jump, -1, 1))
        lx.append(roll(c + half, 1, 1))
        rx.append(c - half)
    (fx,) = stacked_flux([(0, lx)], [(0, rx)])
    return [a - roll(a, -1, 1) for a in fx]


def fine_tendency(q, ghosts):
    lane = lax.broadcasted_iota(jnp.int32, (1, 8, 128), 2)
    row = lax.broadcasted_iota(jnp.int32, (1, 8, 128), 1)
    firsts = (row == 0, lane < 16, lane % 16 == 0)
    lasts = (row == 7, lane >= 112, lane % 16 == 15)
    steps = ((1, 1), (16, 2), (1, 2))
    moves = ((4, 1), (64, 2), (8, 2))
    halves = (row >= 4, lane >= 64, lane % 16 >= 8)

    def shared(fields, axis):
        move, dim = moves[axis]
        return [jnp.where(halves[axis], a[0:1], roll(a[1:2], move, dim)) for a in fields]

    lefts, rights, end_lefts, end_rights = [], [], [], []
    for axis in range(3):
        step, dim = steps[axis]
        left, right, tops = [], [], []
        for f in range(5):
            a = q[f]
            g = ghosts[axis][f]
            before = jnp.where(firsts[axis], g, roll(a, step, dim))
            after = jnp.where(lasts[axis], g, roll(a, -step, dim))
            half = 0.5 * minmod(a - before, after - a)
            up = a + half
            left.append(jnp.where(firsts[axis], g, roll(up, step, dim)))
            right.append(a - half)
            tops.append(up)
        lefts.append((axis, left))
        rights.append((axis, right))
        end_lefts.append((axis, shared(tops, axis)))
        end_rights.append((axis, shared(ghosts[axis], axis)))
    parts = stacked_flux(lefts + end_lefts, rights + end_rights)
    out = [None] * 5
    for axis in range(3):
        step, dim = steps[axis]
        for f in range(5):
            low = parts[axis][f]
            top = parts[3 + axis][f]
            top = jnp.concatenate([top, roll(top, -moves[axis][0], dim)])
            change = jnp.where(lasts[axis], top, roll(low, -step, dim)) - low
            out[f] = -change if out[f] is None else out[f] - change
    return [2.0 * part for part in out]


def kernel(
    sizes,
    density_in,
    velocity_in,
    pressure_in,
    fine_density_in,
    fine_velocity_in,
    fine_pressure_in,
    parents_in,
    shifts_in,
    coarse_out,
    fine_out,
    density,
    velocity,
    pressure,
    fine_density,
    fine_velocity,
    fine_pressure,
    ext,
    xs,
    xr,
    ys,
    yr,
    zs,
    zr,
    xs1,
    xr1,
    ys1,
    yr1,
    yf,
    xf,
    msg,
    got,
    msg_z,
    got_z,
    msg_f,
    got_f,
    mean,
    mean_got,
    laid,
    upd,
    sel,
    expand_t,
    expand_y,
    place,
    parents,
    shifts,
    load_sem,
    send_sem,
    recv_sem,
):
    nx, ny, nz = sizes
    cz = 128
    gx, gy, gz = lax.axis_index("gx"), lax.axis_index("gy"), lax.axis_index("gz")
    x_up, x_dn = {"gx": lax.rem(gx + 1, nx)}, {"gx": lax.rem(gx + nx - 1, nx)}
    y_up, y_dn = {"gy": lax.rem(gy + 1, ny)}, {"gy": lax.rem(gy + ny - 1, ny)}
    column = [lax.rem(gz + d, nz) for d in range(nz)]
    z_up, z_dn = {"gz": column[1]}, {"gz": column[nz - 1]}
    started = []

    def send(src, dst, device):
        at = len(started)
        copy = pltpu.make_async_remote_copy(
            src_ref=src,
            dst_ref=dst,
            send_sem=send_sem.at[at],
            recv_sem=recv_sem.at[at],
            device_id=device,
            device_id_type=MESH,
        )
        copy.start()
        started.append(copy)
        return copy

    loads = []
    for src, dst in (
        (density_in, density),
        (velocity_in, velocity),
        (pressure_in, pressure),
        (parents_in, parents),
        (shifts_in, shifts),
        (fine_density_in, fine_density),
        (fine_velocity_in, fine_velocity),
        (fine_pressure_in, fine_pressure),
    ):
        load = pltpu.make_async_copy(src, dst, load_sem.at[len(loads)])
        load.start()
        loads.append(load)

    barrier = pltpu.get_barrier_semaphore()
    partners = [x_up, x_dn, y_up, y_dn] + [{"gz": column[d]} for d in range(1, nz)]
    for device in partners:
        pl.semaphore_signal(barrier, inc=1, device_id=device, device_id_type=MESH)

    lane1 = lax.broadcasted_iota(jnp.int32, (8, 128), 1)
    lane3 = lax.broadcasted_iota(jnp.int32, (1, 8, 128), 2)

    def pack_z(fields, at):
        packed = jnp.zeros((4, 8, 128), F32)
        for f in range(5):
            packed = jnp.where(lane3 // 4 == f, roll(fields[f], 2 + 4 * f, 2), packed)
        zs[at] = packed

    def start_halos(fields, at):
        pack_z(fields, at)
        for f in range(5):
            xs[at, 0, f] = fields[f][:, 2:4, :]
            xs[at, 1, f] = fields[f][:, 4:6, :]
            ys[at, 0, f] = fields[f][0:2, 2:6, :]
            ys[at, 1, f] = fields[f][2:4, 2:6, :]
        if at == 0:
            pl.semaphore_wait(barrier, len(partners))
        return [
            send(xs.at[at, 1], xr.at[at, 0], x_up),
            send(xs.at[at, 0], xr.at[at, 1], x_dn),
            send(ys.at[at, 1], yr.at[at, 0], y_up),
            send(ys.at[at, 0], yr.at[at, 1], y_dn),
            send(zs.at[at], zr.at[at, 0], z_up),
            send(zs.at[at], zr.at[at, 1], z_dn),
        ]

    def coarse_stage(at, copies):
        for copy in copies[2:6]:
            copy.wait_recv()
        for f in range(5):
            ext[f, 0:2, 2:6, :] = yr[at, 0, f]
            ext[f, 6:8, 2:6, :] = yr[at, 1, f]
        ends = jnp.where(lane3 % 4 < 2, zr[at, 0], zr[at, 1])
        ends = [roll(ends, 126 - 4 * f, 2) for f in range(5)]
        change = coarse_fluxes_yz([ext[f] for f in range(5)], ends)
        for copy in copies[0:2]:
            copy.wait_recv()
        for f in range(5):
            ext[f, 2:6, 0:2, :] = xr[at, 0, f]
            ext[f, 2:6, 6:8, :] = xr[at, 1, f]
        block = [ext[f, 2:6] for f in range(5)]
        change = [a + b for a, b in zip(change, coarse_fluxes_x(block))]
        return block, change

    group = lax.broadcasted_iota(jnp.int32, (48, 128), 1) // 32

    def start_picked(rows, size, out, into):
        copies = []
        for chunk in range((nz + 3) // 4):
            picked = [mm(rows[r], sel[chunk, r]) for r in range(4)]
            for d in range(4 * chunk, min(4 * chunk + 4, nz)):
                body = jnp.zeros((size, 128), F32)
                for r in range(4):
                    body = jnp.where(group[0:size] == (d + r) % 4, picked[r][0:size], body)
                parts = [(0, size, body)]
                total = into.shape[1]
                if total > size:
                    tail = jnp.where(lane1 // 32 == d % 4, picked[0][size:total], 0.0)
                    parts.append((size, total, tail))
                for low, high, part in parts:
                    if d == 0:
                        into[0, low:high, :] = part
                    else:
                        out[d - 1, low:high, :] = part
                if d > 0:
                    copies.append(send(out.at[d - 1], into.at[d], {"gz": column[d]}))
        return copies

    def take_picked(copies, into):
        for copy in copies:
            copy.wait_recv()
        total = into[0]
        for d in range(1, nz):
            total = total + roll(into[d], -32 * (d % 4), 1)
        return total

    def tiles(total, count):
        return [total[8 * k : 8 * k + 8] for k in range(count)]

    def turned(first, last):
        return [roll(first, -32 * f, 1) for f in range(4)] + [last]

    row2 = lax.broadcasted_iota(jnp.int32, (8, 128), 0)

    def doubled(tile, base):
        out = tile[base : base + 1]
        for k in range(1, 4):
            out = jnp.where(row2 >= 2 * k, tile[base + k : base + k + 1], out)
        return jnp.broadcast_to(out, (8, 128))

    def injected(inner, faces):
        rows = [doubled(tile, 2) for tile in inner] + list(inner)
        wide = mm(jnp.concatenate(rows), expand_t[...])
        rows = [doubled(tile, 0) for tile in faces] + [doubled(tile, 4) for tile in faces]
        sides = mm(jnp.concatenate(rows), expand_y[...])

        def both(matrix, first_row, left, right):
            return jnp.stack(
                [
                    matrix[first_row : first_row + 8, left : left + 128],
                    matrix[first_row : first_row + 8, right : right + 128],
                ]
            )

        row = lax.broadcasted_iota(jnp.int32, (1, 8, 128), 1)
        cells, in_x, in_y, in_z = [], [], [], []
        for f in range(5):
            cells.append(both(wide, 8 * f, 0, 128))
            in_z.append(both(wide, 8 * f, 256, 384))
            edge = both(wide, 40 + 8 * f, 0, 128)
            in_x.append(jnp.where(row < 4, edge[:, 1:2, :], edge[:, 6:7, :]))
            low = both(sides, 8 * f, 0, 128)
            high = both(sides, 40 + 8 * f, 0, 128)
            in_y.append(jnp.where(lane3 < 64, low, high))
        return cells, (in_x, in_y, in_z)

    ext[...] = jnp.ones(ext.shape, F32)
    for load in loads[0:3]:
        load.wait()
    for y in range(4):
        ext[0, 2 + y, 2:6, :] = density[:, y, :]
        for k in range(3):
            ext[1 + k, 2 + y, 2:6, :] = velocity[k, :, y, :]
        ext[4, 2 + y, 2:6, :] = pressure[:, y, :]
    halos = start_halos([ext[f, 2:6] for f in range(5)], 0)
    for load in loads[3:8]:
        load.wait()

    big_row = lax.broadcasted_iota(jnp.int32, (128, 128), 0)

    def one_hot(index):
        return jnp.where(big_row == index[0:1, :], 1.0, 0.0).astype(BF16)

    slot = lane1 % 16
    for chunk in range((nz + 3) // 4):
        target = jnp.full((8, 128), -4 * cz * nz, jnp.int32)
        for d in range(4 * chunk, min(4 * chunk + 4, nz)):
            for b in range(2):
                box = 2 * column[d] + b
                low = parents[box] * cz + shifts[box] - 1
                target = jnp.where(lane1 // 16 == 2 * (d % 4) + b, low + slot, target)
        target = jnp.where(target == -1, target + nz * cz, target)
        target = jnp.where(target >= nz * cz, target - nz * cz, target)
        target = jnp.where(slot < 10, target - gz * cz, -1)
        for r in range(4):
            sel[chunk, r] = one_hot(roll(target, 32 * r, 1))
    fine_y, fine_z = lane1 // 16, lane1 % 16
    for b in range(2):
        base = (fine_y // 2) * 32 + 16 * b
        expand_t[:, 128 * b : 128 * b + 128] = one_hot(base + fine_z // 2 + 1)
        expand_t[:, 256 + 128 * b : 384 + 128 * b] = one_hot(base + jnp.where(fine_z < 8, 0, 9))
        expand_y[:, 128 * b : 128 * b + 128] = one_hot(16 * b + fine_z // 2 + 1)
    big_lane = lax.broadcasted_iota(jnp.int32, (128, 128), 1)
    for pair in range((nz + 1) // 2):
        target = jnp.full((128, 128), -4 * cz, jnp.int32)
        for k in range(2):
            d = 2 * pair + k
            if d < nz:
                owner = column[(nz - d) % nz]
                for b in range(2):
                    box = 2 * owner + b
                    low = jnp.where(parents[box] == gz, shifts[box], -4 * cz)
                    target = jnp.where(big_row // 32 == 2 * k + b, low, target)
        hit = big_lane == target + big_row % 8
        for y in range(4):
            place[128 * pair : 128 * pair + 128, 128 * y : 128 * y + 128] = jnp.where(
                hit & ((big_row % 32) // 8 == y), 1.0, 0.0
            ).astype(BF16)
    count = jnp.zeros((8, 128), F32)
    for box in range(2 * nz):
        low = jnp.where(parents[box] == gz, shifts[box], -4 * cz)
        count = count + jnp.where((lane1 >= low) & (lane1 < low + 8), 1.0, 0.0)
    covered = count[0:4] > 0.0
    share = 1.0 / jnp.maximum(count[0:4], 1.0)

    block, change = coarse_stage(0, halos)
    start = to_conserved(block)
    section = [a + DT_COARSE * b for a, b in zip(start, change)]
    section = to_primitive(section)
    halos = start_halos(section, 1)
    for f in range(5):
        yf[f, 0:4, :] = ext[f, 1, 2:6, :]
        yf[f, 4:8, :] = ext[f, 6, 2:6, :]
    rows = []
    for r in range(4):
        rows.append(jnp.concatenate([ext[f, 2 + r] for f in range(5)] + [yf[r], yf[4], yf[4]]))
    windows = start_picked(rows, 48, msg, got)
    for f in range(5):
        ext[f, 2:6, 2:6, :] = section[f][:, 2:6, :]

    block, change = coarse_stage(1, halos)
    section = to_conserved(block)
    for f in range(5):
        new = 0.5 * start[f] + 0.5 * (section[f] + DT_COARSE * change[f])
        upd[f] = new
        xs1[0, f] = new[:, 2:3, :]
        xs1[1, f] = new[:, 5:6, :]
        ys1[0, f] = new[0, 2:6, :]
        ys1[1, f] = new[3, 2:6, :]
    faces_sent = [
        send(xs1.at[1], xr1.at[0], x_up),
        send(xs1.at[0], xr1.at[1], x_dn),
        send(ys1.at[1], yr1.at[0], y_up),
        send(ys1.at[0], yr1.at[1], y_dn),
    ]

    rows = []
    for r in range(4):
        rows.append(jnp.concatenate([upd[f, r] for f in range(5)] + [upd[4, r]]))
    near = start_picked(rows, 40, msg_z, got_z)

    total = take_picked(windows, got)
    old_inner, old_faces = tiles(total, 5), turned(total[40:48], total[48:56])
    cells, ghosts = injected(old_inner, old_faces)
    detail = [fine_density[...]] + [fine_velocity[k] for k in range(3)] + [fine_pressure[...]]
    prim = [a + b for a, b in zip(cells, detail)]
    state = to_conserved(prim)
    rate = fine_tendency(prim, ghosts)
    stage = [a + DT_FINE * b for a, b in zip(state, rate)]

    for copy in faces_sent:
        copy.wait_recv()
    xf[...] = jnp.zeros(xf.shape, F32)
    for f in range(5):
        xf[:, f, :] = xr1[0, f, :, 0, :]
        xf[:, 8 + f, :] = xr1[1, f, :, 0, :]
        yf[f, 0:4, :] = yr1[0, f]
        yf[f, 4:8, :] = yr1[1, f]
    rows = [jnp.concatenate([xf[r], yf[r], yf[4]]) for r in range(4)]
    far = start_picked(rows, 24, msg_f, got_f)

    rate = fine_tendency(to_primitive(stage), ghosts)
    state = [0.5 * a + 0.5 * (b + DT_FINE * c) for a, b, c in zip(state, stage, rate)]

    new_inner = tiles(take_picked(near, got_z), 5)
    total = take_picked(far, got_f)
    for f in range(5):
        side = jnp.where(row2 == 1, total[f : f + 1], total[8 + f : 9 + f])
        new_inner[f] = jnp.where((row2 >= 2) & (row2 < 6), new_inner[f], side)
    new_faces = turned(total[16:24], total[24:32])

    def middle(old, new):
        mixed = [0.5 * (a + b) for a, b in zip(to_conserved(old), new)]
        mixed[0] = jnp.where(mixed[0] == 0.0, 1.0, mixed[0])
        return to_primitive(mixed)

    _, ghosts = injected(middle(old_inner, new_inner), middle(old_faces, new_faces))
    rate = fine_tendency(to_primitive(state), ghosts)
    stage = [a + DT_FINE * b for a, b in zip(state, rate)]
    rate = fine_tendency(to_primitive(stage), ghosts)
    state = [0.5 * a + 0.5 * (b + DT_FINE * c) for a, b, c in zip(state, stage, rate)]

    child = big_row // 32 * 8 + (big_row % 16) // 2
    matrix = jnp.where(big_lane == child, 0.125, 0.0).astype(BF16)
    flat = mm(jnp.concatenate([a[b] for b in range(2) for a in state]), matrix)
    summed = flat[0:40] + roll(flat[40:80], 32, 1)
    summed = summed + roll(summed, -1, 0)
    keep = (row2 % 2 == 0) & (lane1 < 64)
    parts = [jnp.where(keep, tile, 0.0) for tile in tiles(summed, 5)]
    odd = roll(parts[2] + roll(parts[3], 64, 1), 1, 0)
    packed = jnp.concatenate([parts[0] + roll(parts[1], 64, 1) + odd, parts[4]])
    mean[...] = packed
    mean_got[0] = packed
    copies = [send(mean, mean_got.at[d], {"gz": column[d]}) for d in range(1, nz)]
    for f in range(5):
        fine_out[f] = state[f]
    for copy in copies:
        copy.wait_recv()
    rows = []
    for pair in range((nz + 1) // 2):
        here = mean_got[2 * pair]
        there = mean_got[2 * pair + 1] if 2 * pair + 1 < nz else jnp.zeros((16, 128), F32)
        first = jnp.where(lane1 < 64, here[0:8], roll(there[0:8], 64, 1))
        second = jnp.where(lane1 < 64, roll(here[0:8], 64, 1), there[0:8])
        third = jnp.where(lane1 < 64, here[8:16], roll(there[8:16], 64, 1))
        rows.append(jnp.concatenate([first, second, third, third]))
    total = mm(jnp.concatenate(rows, axis=1), place[...])
    for k in range(3):
        for y in range(4):
            laid[k, y] = total[8 * k : 8 * k + 8, 128 * y : 128 * y + 128]
    for f in range(5):
        tile, at = ((0, 0), (1, 0), (0, 1), (1, 1), (2, 0))[f]
        for y in range(4):
            value = laid[tile, y, pl.ds(at, 4, stride=2), :] * share
            coarse_out[f, :, y, :] = jnp.where(covered, value, upd[f, y, 2:6, :])
    for copy in started:
        copy.wait_send()


def hand_over(coarse, fine, coarse_out, fine_out, sems):
    first = pltpu.make_async_copy(coarse, coarse_out, sems.at[0])
    second = pltpu.make_async_copy(fine, fine_out, sems.at[1])
    first.start()
    second.start()
    first.wait()
    second.wait()


def on_device(sizes, density, velocity, pressure, fine_density, fine_velocity, fine_pressure, parent, shift):
    nz = sizes[2]
    fine = fine_density.shape[2:]
    vmem = pl.BlockSpec(memory_space=pltpu.VMEM)
    hbm = pl.BlockSpec(memory_space=pltpu.HBM)
    copies = 16 + 4 * (nz - 1)
    chunks = (nz + 3) // 4
    scratch = [
        density.shape,
        velocity.shape,
        pressure.shape,
        fine,
        (3,) + fine,
        fine,
        (5, 8, 8, 128),
        (2, 2, 5, 4, 2, 128),
        (2, 2, 5, 4, 2, 128),
        (2, 2, 5, 2, 4, 128),
        (2, 2, 5, 2, 4, 128),
        (2, 4, 8, 128),
        (2, 2, 4, 8, 128),
        (2, 5, 4, 1, 128),
        (2, 5, 4, 1, 128),
        (2, 5, 4, 128),
        (2, 5, 4, 128),
        (5, 8, 128),
        (4, 16, 128),
        (nz - 1, 56, 128),
        (nz, 56, 128),
        (nz - 1, 40, 128),
        (nz, 40, 128),
        (nz - 1, 32, 128),
        (nz, 32, 128),
        (16, 128),
        (nz, 16, 128),
        (3, 4, 8, 128),
        (5, 4, 8, 128),
    ]
    matrices = [(chunks, 4, 128, 128), (128, 512), (128, 256), (128 * ((nz + 1) // 2), 512)]
    coarse, fine_state = pl.pallas_call(
        functools.partial(kernel, sizes),
        out_shape=(
            pltpu.VMEM((5,) + density.shape, F32),
            pltpu.VMEM((5,) + fine, F32),
        ),
        in_specs=[hbm] * 8,
        out_specs=(vmem, vmem),
        scratch_shapes=[pltpu.VMEM(shape, F32) for shape in scratch]
        + [pltpu.VMEM(shape, BF16) for shape in matrices]
        + [pltpu.SMEM((2 * nz,), jnp.int32)] * 2
        + [pltpu.SemaphoreType.DMA((8,)), pltpu.SemaphoreType.DMA((copies,)), pltpu.SemaphoreType.DMA((copies,))],
        compiler_params=pltpu.CompilerParams(
            collective_id=0, has_side_effects=True, vmem_limit_bytes=56 * 1024 * 1024
        ),
    )(
        density,
        velocity,
        pressure,
        fine_density.reshape(fine),
        fine_velocity.reshape((3,) + fine),
        fine_pressure.reshape(fine),
        parent.reshape(-1),
        shift.reshape(-1),
    )
    coarse, fine_state = pl.pallas_call(
        hand_over,
        out_shape=(
            jax.ShapeDtypeStruct(coarse.shape, F32),
            jax.ShapeDtypeStruct(fine_state.shape, F32),
        ),
        in_specs=[vmem, vmem],
        out_specs=(hbm, hbm),
        scratch_shapes=[pltpu.SemaphoreType.DMA((2,))],
    )(coarse, fine_state)
    return coarse, fine_state.reshape((5, 1, 1) + fine)


def solution(mesh):
    sizes = tuple(mesh.shape[axis] for axis in ("gx", "gy", "gz"))
    in_specs = (
        P("gx", "gy", "gz"),
        P(None, "gx", "gy", "gz"),
        P("gx", "gy", "gz"),
        P("gx", "gy", "gz", None, None),
        P(None, "gx", "gy", "gz", None, None),
        P("gx", "gy", "gz", None, None),
        P("gx", "gy", None, None),
        P("gx", "gy", None),
    )
    out_specs = (P(None, "gx", "gy", "gz"), P(None, "gx", "gy", "gz", None, None))
    return jax.shard_map(
        functools.partial(on_device, sizes),
        mesh=mesh,
        in_specs=in_specs,
        out_specs=out_specs,
        check_vma=False,
    )
```

```python
import functools

import jax
import jax.numpy as jnp
from jax import lax
from jax.experimental import pallas as pl
from jax.experimental.pallas import tpu as pltpu
from jax.sharding import PartitionSpec as P

GAMMA = 1.4
DT_COARSE = 0.05
DT_FINE = 0.025
MESH = pl.DeviceIdType.MESH
F32 = jnp.float32
BF16 = jnp.bfloat16


def mm(a, b):
    size = a.shape[0]
    high = a.astype(BF16).astype(F32)
    rest = a - high
    middle = rest.astype(BF16).astype(F32)
    parts = jnp.concatenate([high, middle, rest - middle]).astype(BF16)
    out = lax.dot_general(parts, b, (((1,), (0,)), ((), ())), preferred_element_type=F32)
    return (out[0:size] + out[size : 2 * size]) + out[2 * size : 3 * size]


def to_conserved(q):
    rho, u, v, w, p = q
    energy = p * (1.0 / (GAMMA - 1.0)) + 0.5 * rho * (u * u + v * v + w * w)
    return [rho, rho * u, rho * v, rho * w, energy]


def to_primitive(c):
    rho, mx, my, mz, energy = c
    inv = 1.0 / rho
    u, v, w = mx * inv, my * inv, mz * inv
    p = (GAMMA - 1.0) * (energy - 0.5 * (mx * u + my * v + mz * w))
    return [rho, u, v, w, p]


def minmod(a, b):
    return jnp.maximum(jnp.minimum(a, b), 0.0) + jnp.minimum(jnp.maximum(a, b), 0.0)


def hllc(left, right):
    rl, ul, _, _, pl_ = left
    rr, ur, _, _, pr = right
    cl = jnp.sqrt(GAMMA * pl_ / rl)
    cr = jnp.sqrt(GAMMA * pr / rr)
    sl = jnp.minimum(ul - cl, ur - cr)
    sr = jnp.maximum(ul + cl, ur + cr)
    ml = rl * (sl - ul)
    mr = rr * (sr - ur)
    contact = (pr - pl_ + ml * ul - mr * ur) / (ml - mr)
    use_left = (sl >= 0.0) | (contact >= 0.0)
    rho, un, t1, t2, p = [jnp.where(use_left, a, b) for a, b in zip(left, right)]
    wave = jnp.where(use_left, sl, sr)
    mass = jnp.where(use_left, ml, mr)
    outside = (sl >= 0.0) | (jnp.logical_not(use_left) & (sr < 0.0))
    scale = 1.0 / (wave - contact)
    energy = p * (1.0 / (GAMMA - 1.0)) + 0.5 * rho * (un * un + t1 * t1 + t2 * t2)
    star_rho = mass * scale
    star_energy = ((wave - un) * energy + (contact - un) * (mass * contact + p)) * scale
    flow = rho * un
    zero = jnp.zeros_like(rho)
    f0 = flow + jnp.where(outside, zero, wave * (star_rho - rho))
    fn = flow * un + p + jnp.where(outside, zero, wave * (star_rho * contact - flow))
    fe = (energy + p) * un + jnp.where(outside, zero, wave * (star_energy - energy))
    return [f0, fn, t1 * f0, t2 * f0, fe]


TURN = ((0, 1, 2, 3, 4), (0, 2, 3, 1, 4), (0, 3, 1, 2, 4))


def stacked_flux(lefts, rights):
    sizes = [part[0].shape[0] for _, part in lefts]

    def joined(parts):
        return [jnp.concatenate([part[TURN[axis][i]] for axis, part in parts]) for i in range(5)]

    fluxes = hllc(joined(lefts), joined(rights))
    out = []
    at = 0
    for (axis, _), size in zip(lefts, sizes):
        part = [None] * 5
        for i in range(5):
            part[TURN[axis][i]] = fluxes[i][at : at + size]
        out.append(part)
        at += size
    return out


def roll(a, shift, axis):
    size = a.shape[axis]
    shift = shift % size
    return a if shift == 0 else pltpu.roll(a, shift, axis)


def coarse_fluxes_yz(q, n):
    lane = lax.broadcasted_iota(jnp.int32, (1, 8, 128), 2)
    row = lax.broadcasted_iota(jnp.int32, (1, 8, 128), 1)
    inner = (row >= 2) & (row < 6)
    ly, ry, lz, rz = [], [], [], []
    for f in range(5):
        a = q[f]
        jump = a[1:8] - a[0:7]
        half = 0.5 * minmod(jump[0:6], jump[1:7])
        ly.append(a[1:6] + half[0:5])
        ry.append(a[2:7] - half[1:6])
        c = a[2:6]
        g = n[f]
        before = roll(jnp.where(lane == 127, g, c), 1, 2)
        after = roll(jnp.where(lane == 0, g, c), -1, 2)
        half = 0.5 * minmod(c - before, after - c)
        g_before = roll(jnp.where(lane == 127, c, g), 1, 2)
        g_after = roll(jnp.where(lane == 0, c, g), -1, 2)
        g_half = 0.5 * minmod(g - g_before, g_after - g)
        up = c + half
        down = c - half
        low_left = roll(jnp.where(lane == 127, g + g_half, up), 1, 2)
        high_right = roll(jnp.where(lane == 0, g - g_half, down), -1, 2)
        lz.append(jnp.where(inner, low_left, roll(up, 4, 1)))
        rz.append(jnp.where(inner, down, roll(high_right, 4, 1)))
    fy, fz = stacked_flux([(1, ly), (2, lz)], [(1, ry), (2, rz)])
    out = []
    for f in range(5):
        dy = fy[f][1:5] - fy[f][0:4]
        dz = roll(fz[f], 4, 1) - fz[f]
        out.append(-dy - dz)
    return out


def coarse_fluxes_x(q):
    lx, rx = [], []
    for c in q:
        jump = c - roll(c, 1, 1)
        half = 0.5 * minmod(jump, roll(jump, -1, 1))
        lx.append(roll(c + half, 1, 1))
        rx.append(c - half)
    (fx,) = stacked_flux([(0, lx)], [(0, rx)])
    return [a - roll(a, -1, 1) for a in fx]


def fine_tendency(q, ghosts):
    lane = lax.broadcasted_iota(jnp.int32, (1, 8, 128), 2)
    row = lax.broadcasted_iota(jnp.int32, (1, 8, 128), 1)
    firsts = (row == 0, lane < 16, lane % 16 == 0)
    lasts = (row == 7, lane >= 112, lane % 16 == 15)
    steps = ((1, 1), (16, 2), (1, 2))
    moves = ((4, 1), (64, 2), (8, 2))
    halves = (row >= 4, lane >= 64, lane % 16 >= 8)

    def shared(fields, axis):
        move, dim = moves[axis]
        return [jnp.where(halves[axis], a[0:1], roll(a[1:2], move, dim)) for a in fields]

    lefts, rights, end_lefts, end_rights = [], [], [], []
    for axis in range(3):
        step, dim = steps[axis]
        left, right, tops = [], [], []
        for f in range(5):
            a = q[f]
            g = ghosts[axis][f]
            before = jnp.where(firsts[axis], g, roll(a, step, dim))
            after = jnp.where(lasts[axis], g, roll(a, -step, dim))
            half = 0.5 * minmod(a - before, after - a)
            up = a + half
            left.append(jnp.where(firsts[axis], g, roll(up, step, dim)))
            right.append(a - half)
            tops.append(up)
        lefts.append((axis, left))
        rights.append((axis, right))
        end_lefts.append((axis, shared(tops, axis)))
        end_rights.append((axis, shared(ghosts[axis], axis)))
    parts = stacked_flux(lefts + end_lefts, rights + end_rights)
    out = [None] * 5
    for axis in range(3):
        step, dim = steps[axis]
        for f in range(5):
            low = parts[axis][f]
            top = parts[3 + axis][f]
            top = jnp.concatenate([top, roll(top, -moves[axis][0], dim)])
            change = jnp.where(lasts[axis], top, roll(low, -step, dim)) - low
            out[f] = -change if out[f] is None else out[f] - change
    return [2.0 * part for part in out]


def kernel(
    sizes,
    density_in,
    velocity_in,
    pressure_in,
    fine_density_in,
    fine_velocity_in,
    fine_pressure_in,
    parents_in,
    shifts_in,
    coarse_out,
    fine_out,
    density,
    velocity,
    pressure,
    fine_density,
    fine_velocity,
    fine_pressure,
    ext,
    xs,
    xr,
    ys,
    yr,
    zs,
    zr,
    xs1,
    xr1,
    ys1,
    yr1,
    yf,
    xf,
    msg,
    got,
    msg_z,
    got_z,
    msg_f,
    got_f,
    mean,
    mean_got,
    laid,
    upd,
    win,
    rim,
    now,
    sel,
    expand_t,
    expand_y,
    place,
    parents,
    shifts,
    load_sem,
    send_sem,
    recv_sem,
):
    nx, ny, nz = sizes
    cz = 128
    gx, gy, gz = lax.axis_index("gx"), lax.axis_index("gy"), lax.axis_index("gz")
    x_up, x_dn = {"gx": lax.rem(gx + 1, nx)}, {"gx": lax.rem(gx + nx - 1, nx)}
    y_up, y_dn = {"gy": lax.rem(gy + 1, ny)}, {"gy": lax.rem(gy + ny - 1, ny)}
    column = [lax.rem(gz + d, nz) for d in range(nz)]
    z_up, z_dn = {"gz": column[1]}, {"gz": column[nz - 1]}
    started = []

    def remote(src, dst, device, at):
        return pltpu.make_async_remote_copy(
            src_ref=src,
            dst_ref=dst,
            send_sem=send_sem.at[at],
            recv_sem=recv_sem.at[at],
            device_id=device,
            device_id_type=MESH,
        )

    def planned(src, dst, device):
        copy = remote(src, dst, device, 12 + len(started))
        started.append(copy)
        return copy

    def halo_copies(at):
        pairs = [
            (xs.at[at, 1], xr.at[at, 0], x_up),
            (xs.at[at, 0], xr.at[at, 1], x_dn),
            (ys.at[at, 1], yr.at[at, 0], y_up),
            (ys.at[at, 0], yr.at[at, 1], y_dn),
            (zs.at[at], zr.at[at, 0], z_up),
            (zs.at[at], zr.at[at, 1], z_dn),
        ]
        return [remote(*pair, 6 * at + k) for k, pair in enumerate(pairs)]

    def to_column(out, into):
        return [planned(out.at[d - 1], into.at[d], {"gz": column[d]}) for d in range(1, nz)]

    windows, near, far = to_column(msg, got), to_column(msg_z, got_z), to_column(msg_f, got_f)
    faces_sent = [
        planned(xs1.at[1], xr1.at[0], x_up),
        planned(xs1.at[0], xr1.at[1], x_dn),
        planned(ys1.at[1], yr1.at[0], y_up),
        planned(ys1.at[0], yr1.at[1], y_dn),
    ]
    means_sent = [planned(mean, mean_got.at[d], {"gz": column[d]}) for d in range(1, nz)]

    loads = []
    for src, dst in (
        (density_in, density),
        (velocity_in, velocity),
        (pressure_in, pressure),
        (parents_in, parents),
        (shifts_in, shifts),
        (fine_density_in, fine_density),
        (fine_velocity_in, fine_velocity),
        (fine_pressure_in, fine_pressure),
    ):
        load = pltpu.make_async_copy(src, dst, load_sem.at[len(loads)])
        load.start()
        loads.append(load)

    barrier = pltpu.get_barrier_semaphore()
    partners = [x_up, x_dn, y_up, y_dn] + [{"gz": column[d]} for d in range(1, nz)]
    for device in partners:
        pl.semaphore_signal(barrier, inc=1, device_id=device, device_id_type=MESH)

    lane1 = lax.broadcasted_iota(jnp.int32, (8, 128), 1)
    lane3 = lax.broadcasted_iota(jnp.int32, (1, 8, 128), 2)

    def pack_z(fields, at):
        packed = jnp.zeros((4, 8, 128), F32)
        for f in range(5):
            packed = jnp.where(lane3 // 4 == f, roll(fields[f], 2 + 4 * f, 2), packed)
        zs[at] = packed

    def start_halos(fields, at):
        pack_z(fields, at)
        for f in range(5):
            xs[at, 0, f] = fields[f][:, 2:4, :]
            xs[at, 1, f] = fields[f][:, 4:6, :]
            ys[at, 0, f] = fields[f][0:2, 2:6, :]
            ys[at, 1, f] = fields[f][2:4, 2:6, :]
        if at == 0:
            pl.semaphore_wait(barrier, len(partners))
        for copy in halo_copies(at):
            copy.start()

    def coarse_stage(at):
        copies = halo_copies(at)
        for copy in copies[2:6]:
            copy.wait_recv()
        for f in range(5):
            ext[f, 0:2, 2:6, :] = yr[at, 0, f]
            ext[f, 6:8, 2:6, :] = yr[at, 1, f]
        ends = jnp.where(lane3 % 4 < 2, zr[at, 0], zr[at, 1])
        ends = [roll(ends, 126 - 4 * f, 2) for f in range(5)]
        change = coarse_fluxes_yz([ext[f] for f in range(5)], ends)
        for copy in copies[0:2]:
            copy.wait_recv()
        for f in range(5):
            ext[f, 2:6, 0:2, :] = xr[at, 0, f]
            ext[f, 2:6, 6:8, :] = xr[at, 1, f]
        block = [ext[f, 2:6] for f in range(5)]
        change = [a + b for a, b in zip(change, coarse_fluxes_x(block))]
        return block, change

    group = lax.broadcasted_iota(jnp.int32, (48, 128), 1) // 32

    def start_picked(rows, size, out, into, copies):
        for chunk in range((nz + 3) // 4):
            picked = [mm(rows[r], sel[chunk, r]) for r in range(4)]
            for d in range(4 * chunk, min(4 * chunk + 4, nz)):
                body = jnp.zeros((size, 128), F32)
                for r in range(4):
                    body = jnp.where(group[0:size] == (d + r) % 4, picked[r][0:size], body)
                parts = [(0, size, body)]
                total = into.shape[1]
                if total > size:
                    tail = jnp.where(lane1 // 32 == d % 4, picked[0][size:total], 0.0)
                    parts.append((size, total, tail))
                for low, high, part in parts:
                    if d == 0:
                        into[0, low:high, :] = part
                    else:
                        out[d - 1, low:high, :] = part
                if d > 0:
                    copies[d - 1].start()

    def take_picked(copies, into):
        for copy in copies:
            copy.wait_recv()
        total = into[0]
        for d in range(1, nz):
            total = total + roll(into[d], -32 * (d % 4), 1)
        return total

    def tiles(total, count):
        return [total[8 * k : 8 * k + 8] for k in range(count)]

    def turned(first, last):
        return [roll(first, -32 * f, 1) for f in range(4)] + [last]

    row2 = lax.broadcasted_iota(jnp.int32, (8, 128), 0)

    def doubled(tile, base):
        out = tile[base : base + 1]
        for k in range(1, 4):
            out = jnp.where(row2 >= 2 * k, tile[base + k : base + k + 1], out)
        return jnp.broadcast_to(out, (8, 128))

    def injected(inner, faces):
        rows = [doubled(tile, 2) for tile in inner] + list(inner)
        wide = mm(jnp.concatenate(rows), expand_t[...])
        rows = [doubled(tile, 0) for tile in faces] + [doubled(tile, 4) for tile in faces]
        sides = mm(jnp.concatenate(rows), expand_y[...])

        def both(matrix, first_row, left, right):
            return jnp.stack(
                [
                    matrix[first_row : first_row + 8, left : left + 128],
                    matrix[first_row : first_row + 8, right : right + 128],
                ]
            )

        row = lax.broadcasted_iota(jnp.int32, (1, 8, 128), 1)
        cells, in_x, in_y, in_z = [], [], [], []
        for f in range(5):
            cells.append(both(wide, 8 * f, 0, 128))
            in_z.append(both(wide, 8 * f, 256, 384))
            edge = both(wide, 40 + 8 * f, 0, 128)
            in_x.append(jnp.where(row < 4, edge[:, 1:2, :], edge[:, 6:7, :]))
            low = both(sides, 8 * f, 0, 128)
            high = both(sides, 40 + 8 * f, 0, 128)
            in_y.append(jnp.where(lane3 < 64, low, high))
        return cells, (in_x, in_y, in_z)

    ext[...] = jnp.ones(ext.shape, F32)
    for load in loads[0:3]:
        load.wait()
    for y in range(4):
        ext[0, 2 + y, 2:6, :] = density[:, y, :]
        for k in range(3):
            ext[1 + k, 2 + y, 2:6, :] = velocity[k, :, y, :]
        ext[4, 2 + y, 2:6, :] = pressure[:, y, :]
    start_halos([ext[f, 2:6] for f in range(5)], 0)
    for load in loads[3:8]:
        load.wait()

    big_row = lax.broadcasted_iota(jnp.int32, (128, 128), 0)

    def one_hot(index):
        return jnp.where(big_row == index[0:1, :], 1.0, 0.0).astype(BF16)

    slot = lane1 % 16
    for chunk in range((nz + 3) // 4):
        target = jnp.full((8, 128), -4 * cz * nz, jnp.int32)
        for d in range(4 * chunk, min(4 * chunk + 4, nz)):
            for b in range(2):
                box = 2 * column[d] + b
                low = parents[box] * cz + shifts[box] - 1
                target = jnp.where(lane1 // 16 == 2 * (d % 4) + b, low + slot, target)
        target = jnp.where(target == -1, target + nz * cz, target)
        target = jnp.where(target >= nz * cz, target - nz * cz, target)
        target = jnp.where(slot < 10, target - gz * cz, -1)
        for r in range(4):
            sel[chunk, r] = one_hot(roll(target, 32 * r, 1))
    fine_y, fine_z = lane1 // 16, lane1 % 16
    for b in range(2):
        base = (fine_y // 2) * 32 + 16 * b
        expand_t[:, 128 * b : 128 * b + 128] = one_hot(base + fine_z // 2 + 1)
        expand_t[:, 256 + 128 * b : 384 + 128 * b] = one_hot(base + jnp.where(fine_z < 8, 0, 9))
        expand_y[:, 128 * b : 128 * b + 128] = one_hot(16 * b + fine_z // 2 + 1)
    big_lane = lax.broadcasted_iota(jnp.int32, (128, 128), 1)
    for pair in range((nz + 1) // 2):
        target = jnp.full((128, 128), -4 * cz, jnp.int32)
        for k in range(2):
            d = 2 * pair + k
            if d < nz:
                owner = column[(nz - d) % nz]
                for b in range(2):
                    box = 2 * owner + b
                    low = jnp.where(parents[box] == gz, shifts[box], -4 * cz)
                    target = jnp.where(big_row // 32 == 2 * k + b, low, target)
        hit = big_lane == target + big_row % 8
        for y in range(4):
            place[128 * pair : 128 * pair + 128, 128 * y : 128 * y + 128] = jnp.where(
                hit & ((big_row % 32) // 8 == y), 1.0, 0.0
            ).astype(BF16)
    count = jnp.zeros((8, 128), F32)
    for box in range(2 * nz):
        low = jnp.where(parents[box] == gz, shifts[box], -4 * cz)
        count = count + jnp.where((lane1 >= low) & (lane1 < low + 8), 1.0, 0.0)
    covered = count[0:4] > 0.0
    share = 1.0 / jnp.maximum(count[0:4], 1.0)

    @pl.loop(0, 2)
    def _(at):
        block, change = coarse_stage(at)
        base = to_conserved(block)
        moved = [a + DT_COARSE * b for a, b in zip(base, change)]

        @pl.when(at == 0)
        def _():
            section = to_primitive(moved)
            start_halos(section, 1)
            for f in range(5):
                upd[f] = base[f]
                yf[f, 0:4, :] = ext[f, 1, 2:6, :]
                yf[f, 4:8, :] = ext[f, 6, 2:6, :]
            rows = []
            for r in range(4):
                rows.append(
                    jnp.concatenate([ext[f, 2 + r] for f in range(5)] + [yf[r], yf[4], yf[4]])
                )
            start_picked(rows, 48, msg, got, windows)
            for f in range(5):
                ext[f, 2:6, 2:6, :] = section[f][:, 2:6, :]

        @pl.when(at == 1)
        def _():
            for f in range(5):
                new = 0.5 * upd[f] + 0.5 * moved[f]
                upd[f] = new
                xs1[0, f] = new[:, 2:3, :]
                xs1[1, f] = new[:, 5:6, :]
                ys1[0, f] = new[0, 2:6, :]
                ys1[1, f] = new[3, 2:6, :]
            for copy in faces_sent:
                copy.start()

    rows = []
    for r in range(4):
        rows.append(jnp.concatenate([upd[f, r] for f in range(5)] + [upd[4, r]]))
    start_picked(rows, 40, msg_z, got_z, near)

    total = take_picked(windows, got)
    for f, tile in enumerate(tiles(total, 5) + turned(total[40:48], total[48:56])):
        win[f] = tile

    def middle(old, new):
        mixed = [0.5 * (a + b) for a, b in zip(to_conserved(old), new)]
        mixed[0] = jnp.where(mixed[0] == 0.0, 1.0, mixed[0])
        return to_primitive(mixed)

    @pl.loop(0, 4)
    def _(step):
        @pl.when(step % 2 == 0)
        def _():
            cells, ghosts = injected([win[f] for f in range(5)], [win[5 + f] for f in range(5)])
            for axis in range(3):
                for f in range(5):
                    rim[axis, f] = ghosts[axis][f]

            @pl.when(step == 0)
            def _():
                detail = [fine_density[...]] + [fine_velocity[k] for k in range(3)]
                detail.append(fine_pressure[...])
                first = to_conserved([a + b for a, b in zip(cells, detail)])
                for f in range(5):
                    fine_out[f] = first[f]
                    now[f] = first[f]

        current = [now[f] for f in range(5)]
        ghosts = [[rim[axis, f] for f in range(5)] for axis in range(3)]
        rate = fine_tendency(to_primitive(current), ghosts)
        kept = jnp.where(step % 2 == 0, 0.0, 0.5)
        state = [
            kept * fine_out[f] + (1.0 - kept) * (current[f] + DT_FINE * rate[f]) for f in range(5)
        ]
        for f in range(5):
            now[f] = state[f]

        @pl.when(step % 2 == 1)
        def _():
            for f in range(5):
                fine_out[f] = state[f]

        @pl.when(step == 0)
        def _():
            for copy in faces_sent:
                copy.wait_recv()
            xf[...] = jnp.zeros(xf.shape, F32)
            for f in range(5):
                xf[:, f, :] = xr1[0, f, :, 0, :]
                xf[:, 8 + f, :] = xr1[1, f, :, 0, :]
                yf[f, 0:4, :] = yr1[0, f]
                yf[f, 4:8, :] = yr1[1, f]
            rows = [jnp.concatenate([xf[r], yf[r], yf[4]]) for r in range(4)]
            start_picked(rows, 24, msg_f, got_f, far)

        @pl.when(step == 1)
        def _():
            new_inner = tiles(take_picked(near, got_z), 5)
            total = take_picked(far, got_f)
            for f in range(5):
                side = jnp.where(row2 == 1, total[f : f + 1], total[8 + f : 9 + f])
                new_inner[f] = jnp.where((row2 >= 2) & (row2 < 6), new_inner[f], side)
            inner = middle([win[f] for f in range(5)], new_inner)
            sides = middle([win[5 + f] for f in range(5)], turned(total[16:24], total[24:32]))
            for f in range(5):
                win[f] = inner[f]
                win[5 + f] = sides[f]

    state = [now[f] for f in range(5)]

    child = big_row // 32 * 8 + (big_row % 16) // 2
    matrix = jnp.where(big_lane == child, 0.125, 0.0).astype(BF16)
    flat = mm(jnp.concatenate([a[b] for b in range(2) for a in state]), matrix)
    summed = flat[0:40] + roll(flat[40:80], 32, 1)
    summed = summed + roll(summed, -1, 0)
    keep = (row2 % 2 == 0) & (lane1 < 64)
    parts = [jnp.where(keep, tile, 0.0) for tile in tiles(summed, 5)]
    odd = roll(parts[2] + roll(parts[3], 64, 1), 1, 0)
    packed = jnp.concatenate([parts[0] + roll(parts[1], 64, 1) + odd, parts[4]])
    mean[...] = packed
    mean_got[0] = packed
    for copy in means_sent:
        copy.start()
    for copy in means_sent:
        copy.wait_recv()
    rows = []
    for pair in range((nz + 1) // 2):
        here = mean_got[2 * pair]
        there = mean_got[2 * pair + 1] if 2 * pair + 1 < nz else jnp.zeros((16, 128), F32)
        first = jnp.where(lane1 < 64, here[0:8], roll(there[0:8], 64, 1))
        second = jnp.where(lane1 < 64, roll(here[0:8], 64, 1), there[0:8])
        third = jnp.where(lane1 < 64, here[8:16], roll(there[8:16], 64, 1))
        rows.append(jnp.concatenate([first, second, third, third]))
    total = mm(jnp.concatenate(rows, axis=1), place[...])
    for k in range(3):
        for y in range(4):
            laid[k, y] = total[8 * k : 8 * k + 8, 128 * y : 128 * y + 128]
    for f in range(5):
        tile, at = ((0, 0), (1, 0), (0, 1), (1, 1), (2, 0))[f]
        for y in range(4):
            value = laid[tile, y, pl.ds(at, 4, stride=2), :] * share
            coarse_out[f, :, y, :] = jnp.where(covered, value, upd[f, y, 2:6, :])
    for copy in halo_copies(0) + halo_copies(1) + started:
        copy.wait_send()


def on_device(sizes, density, velocity, pressure, fine_density, fine_velocity, fine_pressure, parent, shift):
    nz = sizes[2]
    fine = fine_density.shape[2:]
    vmem = pl.BlockSpec(memory_space=pltpu.VMEM)
    hbm = pl.BlockSpec(memory_space=pltpu.HBM)
    copies = 16 + 4 * (nz - 1)
    chunks = (nz + 3) // 4
    scratch = [
        density.shape,
        velocity.shape,
        pressure.shape,
        fine,
        (3,) + fine,
        fine,
        (5, 8, 8, 128),
        (2, 2, 5, 4, 2, 128),
        (2, 2, 5, 4, 2, 128),
        (2, 2, 5, 2, 4, 128),
        (2, 2, 5, 2, 4, 128),
        (2, 4, 8, 128),
        (2, 2, 4, 8, 128),
        (2, 5, 4, 1, 128),
        (2, 5, 4, 1, 128),
        (2, 5, 4, 128),
        (2, 5, 4, 128),
        (5, 8, 128),
        (4, 16, 128),
        (nz - 1, 56, 128),
        (nz, 56, 128),
        (nz - 1, 40, 128),
        (nz, 40, 128),
        (nz - 1, 32, 128),
        (nz, 32, 128),
        (16, 128),
        (nz, 16, 128),
        (3, 4, 8, 128),
        (5, 4, 8, 128),
        (10, 8, 128),
        (3, 5) + fine,
        (5,) + fine,
    ]
    matrices = [(chunks, 4, 128, 128), (128, 512), (128, 256), (128 * ((nz + 1) // 2), 512)]
    coarse, fine_state = pl.pallas_call(
        functools.partial(kernel, sizes),
        out_shape=(
            pltpu.VMEM((5,) + density.shape, F32),
            pltpu.VMEM((5,) + fine, F32),
        ),
        in_specs=[hbm] * 8,
        out_specs=(vmem, vmem),
        scratch_shapes=[pltpu.VMEM(shape, F32) for shape in scratch]
        + [pltpu.VMEM(shape, BF16) for shape in matrices]
        + [pltpu.SMEM((2 * nz,), jnp.int32)] * 2
        + [pltpu.SemaphoreType.DMA((8,)), pltpu.SemaphoreType.DMA((copies,)), pltpu.SemaphoreType.DMA((copies,))],
        compiler_params=pltpu.CompilerParams(
            collective_id=0, has_side_effects=True, vmem_limit_bytes=56 * 1024 * 1024
        ),
    )(
        density,
        velocity,
        pressure,
        fine_density.reshape(fine),
        fine_velocity.reshape((3,) + fine),
        fine_pressure.reshape(fine),
        parent.reshape(-1),
        shift.reshape(-1),
    )
    return coarse, fine_state.reshape((5, 1, 1) + fine)


def solution(mesh):
    sizes = tuple(mesh.shape[axis] for axis in ("gx", "gy", "gz"))
    in_specs = (
        P("gx", "gy", "gz"),
        P(None, "gx", "gy", "gz"),
        P("gx", "gy", "gz"),
        P("gx", "gy", "gz", None, None),
        P(None, "gx", "gy", "gz", None, None),
        P("gx", "gy", "gz", None, None),
        P("gx", "gy", None, None),
        P("gx", "gy", None),
    )
    out_specs = (P(None, "gx", "gy", "gz"), P(None, "gx", "gy", "gz", None, None))
    return jax.shard_map(
        functools.partial(on_device, sizes),
        mesh=mesh,
        in_specs=in_specs,
        out_specs=out_specs,
        check_vma=False,
    )
```

```python
import functools

import jax
import jax.numpy as jnp
from jax import lax
from jax.experimental import pallas as pl
from jax.experimental.pallas import tpu as pltpu
from jax.sharding import PartitionSpec as P

GAMMA = 1.4
DT_COARSE = 0.05
DT_FINE = 0.025
TINY = 1e-30
MESH = pl.DeviceIdType.MESH
F32 = jnp.float32
BF16 = jnp.bfloat16


def mm(a, b):
    size = a.shape[0]
    high = a.astype(BF16).astype(F32)
    rest = a - high
    middle = rest.astype(BF16).astype(F32)
    parts = jnp.concatenate([high, middle, rest - middle]).astype(BF16)
    out = lax.dot_general(parts, b, (((1,), (0,)), ((), ())), preferred_element_type=F32)
    return (out[0:size] + out[size : 2 * size]) + out[2 * size : 3 * size]


def inverse(a):
    near = pl.reciprocal(a, approx=True)
    return near * (2.0 - a * near)


def to_conserved(q):
    rho, u, v, w, p = q
    energy = p * (1.0 / (GAMMA - 1.0)) + 0.5 * rho * (u * u + v * v + w * w)
    return [rho, rho * u, rho * v, rho * w, energy]


def to_primitive(c):
    rho, mx, my, mz, energy = c
    inv = inverse(rho)
    u, v, w = mx * inv, my * inv, mz * inv
    p = (GAMMA - 1.0) * (energy - 0.5 * (mx * u + my * v + mz * w))
    return [rho, u, v, w, p]


def minmod(a, b):
    return jnp.maximum(jnp.minimum(a, b), 0.0) + jnp.minimum(jnp.maximum(a, b), 0.0)


def hllc(left, right):
    rl, ul, _, _, pl_ = left
    rr, ur, _, _, pr = right
    sound_l = GAMMA * pl_ * inverse(rl)
    sound_r = GAMMA * pr * inverse(rr)
    cl = sound_l * lax.rsqrt(jnp.maximum(sound_l, TINY))
    cr = sound_r * lax.rsqrt(jnp.maximum(sound_r, TINY))
    sl = jnp.minimum(ul - cl, ur - cr)
    sr = jnp.maximum(ul + cl, ur + cr)
    ml = rl * (sl - ul)
    mr = rr * (sr - ur)
    contact = (pr - pl_ + ml * ul - mr * ur) * inverse(ml - mr)
    use_left = (sl >= 0.0) | (contact >= 0.0)
    rho, un, t1, t2, p = [jnp.where(use_left, a, b) for a, b in zip(left, right)]
    wave = jnp.where(use_left, sl, sr)
    mass = jnp.where(use_left, ml, mr)
    outside = (sl >= 0.0) | (jnp.logical_not(use_left) & (sr < 0.0))
    scale = inverse(wave - contact)
    energy = p * (1.0 / (GAMMA - 1.0)) + 0.5 * rho * (un * un + t1 * t1 + t2 * t2)
    star_rho = mass * scale
    star_energy = ((wave - un) * energy + (contact - un) * (mass * contact + p)) * scale
    flow = rho * un
    zero = jnp.zeros_like(rho)
    f0 = flow + jnp.where(outside, zero, wave * (star_rho - rho))
    fn = flow * un + p + jnp.where(outside, zero, wave * (star_rho * contact - flow))
    fe = (energy + p) * un + jnp.where(outside, zero, wave * (star_energy - energy))
    return [f0, fn, t1 * f0, t2 * f0, fe]


TURN = ((0, 1, 2, 3, 4), (0, 2, 3, 1, 4), (0, 3, 1, 2, 4))


def stacked_flux(lefts, rights):
    sizes = [part[0].shape[0] for _, part in lefts]

    def joined(parts):
        return [jnp.concatenate([part[TURN[axis][i]] for axis, part in parts]) for i in range(5)]

    fluxes = hllc(joined(lefts), joined(rights))
    out = []
    at = 0
    for (axis, _), size in zip(lefts, sizes):
        part = [None] * 5
        for i in range(5):
            part[TURN[axis][i]] = fluxes[i][at : at + size]
        out.append(part)
        at += size
    return out


def roll(a, shift, axis):
    size = a.shape[axis]
    shift = shift % size
    return a if shift == 0 else pltpu.roll(a, shift, axis)


def coarse_fluxes_yz(q, n):
    lane = lax.broadcasted_iota(jnp.int32, (1, 8, 128), 2)
    row = lax.broadcasted_iota(jnp.int32, (1, 8, 128), 1)
    inner = (row >= 2) & (row < 6)
    ly, ry, lz, rz = [], [], [], []
    for f in range(5):
        a = q[f]
        jump = a[1:8] - a[0:7]
        half = 0.5 * minmod(jump[0:6], jump[1:7])
        ly.append(a[1:6] + half[0:5])
        ry.append(a[2:7] - half[1:6])
        c = a[2:6]
        g = n[f]
        before = roll(jnp.where(lane == 127, g, c), 1, 2)
        after = roll(jnp.where(lane == 0, g, c), -1, 2)
        half = 0.5 * minmod(c - before, after - c)
        g_before = roll(jnp.where(lane == 127, c, g), 1, 2)
        g_after = roll(jnp.where(lane == 0, c, g), -1, 2)
        g_half = 0.5 * minmod(g - g_before, g_after - g)
        up = c + half
        down = c - half
        low_left = roll(jnp.where(lane == 127, g + g_half, up), 1, 2)
        high_right = roll(jnp.where(lane == 0, g - g_half, down), -1, 2)
        lz.append(jnp.where(inner, low_left, roll(up, 4, 1)))
        rz.append(jnp.where(inner, down, roll(high_right, 4, 1)))
    fy, fz = stacked_flux([(1, ly), (2, lz)], [(1, ry), (2, rz)])
    out = []
    for f in range(5):
        dy = fy[f][1:5] - fy[f][0:4]
        dz = roll(fz[f], 4, 1) - fz[f]
        out.append(-dy - dz)
    return out


def coarse_fluxes_x(q):
    lx, rx = [], []
    for c in q:
        jump = c - roll(c, 1, 1)
        half = 0.5 * minmod(jump, roll(jump, -1, 1))
        lx.append(roll(c + half, 1, 1))
        rx.append(c - half)
    (fx,) = stacked_flux([(0, lx)], [(0, rx)])
    return [a - roll(a, -1, 1) for a in fx]


def fine_tendency(q, ghosts):
    lane = lax.broadcasted_iota(jnp.int32, (1, 8, 128), 2)
    row = lax.broadcasted_iota(jnp.int32, (1, 8, 128), 1)
    firsts = (row == 0, lane < 16, lane % 16 == 0)
    lasts = (row == 7, lane >= 112, lane % 16 == 15)
    steps = ((1, 1), (16, 2), (1, 2))
    moves = ((4, 1), (64, 2), (8, 2))
    halves = (row >= 4, lane >= 64, lane % 16 >= 8)

    def shared(fields, axis):
        move, dim = moves[axis]
        return [jnp.where(halves[axis], a[0:1], roll(a[1:2], move, dim)) for a in fields]

    lefts, rights, end_lefts, end_rights = [], [], [], []
    for axis in range(3):
        step, dim = steps[axis]
        left, right, tops = [], [], []
        for f in range(5):
            a = q[f]
            g = ghosts[axis][f]
            before = jnp.where(firsts[axis], g, roll(a, step, dim))
            after = jnp.where(lasts[axis], g, roll(a, -step, dim))
            half = 0.5 * minmod(a - before, after - a)
            up = a + half
            left.append(jnp.where(firsts[axis], g, roll(up, step, dim)))
            right.append(a - half)
            tops.append(up)
        lefts.append((axis, left))
        rights.append((axis, right))
        end_lefts.append((axis, shared(tops, axis)))
        end_rights.append((axis, shared(ghosts[axis], axis)))
    parts = stacked_flux(lefts + end_lefts, rights + end_rights)
    out = [None] * 5
    for axis in range(3):
        step, dim = steps[axis]
        for f in range(5):
            low = parts[axis][f]
            top = parts[3 + axis][f]
            top = jnp.concatenate([top, roll(top, -moves[axis][0], dim)])
            change = jnp.where(lasts[axis], top, roll(low, -step, dim)) - low
            out[f] = -change if out[f] is None else out[f] - change
    return [2.0 * part for part in out]


def kernel(
    sizes,
    density_in,
    velocity_in,
    pressure_in,
    fine_density_in,
    fine_velocity_in,
    fine_pressure_in,
    parents_in,
    shifts_in,
    coarse_out,
    fine_out,
    density,
    velocity,
    pressure,
    fine_density,
    fine_velocity,
    fine_pressure,
    ext,
    xs,
    xr,
    ys,
    yr,
    zs,
    zr,
    xs1,
    xr1,
    ys1,
    yr1,
    yf,
    xf,
    msg,
    got,
    msg_z,
    got_z,
    msg_f,
    got_f,
    mean,
    mean_got,
    laid,
    upd,
    win,
    rim,
    now,
    sel,
    expand_t,
    expand_y,
    place,
    parents,
    shifts,
    load_sem,
    send_sem,
    recv_sem,
):
    nx, ny, nz = sizes
    cz = 128
    gx, gy, gz = lax.axis_index("gx"), lax.axis_index("gy"), lax.axis_index("gz")
    x_up, x_dn = {"gx": lax.rem(gx + 1, nx)}, {"gx": lax.rem(gx + nx - 1, nx)}
    y_up, y_dn = {"gy": lax.rem(gy + 1, ny)}, {"gy": lax.rem(gy + ny - 1, ny)}
    column = [lax.rem(gz + d, nz) for d in range(nz)]
    z_up, z_dn = {"gz": column[1]}, {"gz": column[nz - 1]}
    started = []

    def remote(src, dst, device, at):
        return pltpu.make_async_remote_copy(
            src_ref=src,
            dst_ref=dst,
            send_sem=send_sem.at[at],
            recv_sem=recv_sem.at[at],
            device_id=device,
            device_id_type=MESH,
        )

    def planned(src, dst, device):
        copy = remote(src, dst, device, 12 + len(started))
        started.append(copy)
        return copy

    def halo_copies(at):
        pairs = [
            (xs.at[at, 1], xr.at[at, 0], x_up),
            (xs.at[at, 0], xr.at[at, 1], x_dn),
            (ys.at[at, 1], yr.at[at, 0], y_up),
            (ys.at[at, 0], yr.at[at, 1], y_dn),
            (zs.at[at], zr.at[at, 0], z_up),
            (zs.at[at], zr.at[at, 1], z_dn),
        ]
        return [remote(*pair, 6 * at + k) for k, pair in enumerate(pairs)]

    def to_column(out, into):
        return [planned(out.at[d - 1], into.at[d], {"gz": column[d]}) for d in range(1, nz)]

    windows, near, far = to_column(msg, got), to_column(msg_z, got_z), to_column(msg_f, got_f)
    faces_sent = [
        planned(xs1.at[1], xr1.at[0], x_up),
        planned(xs1.at[0], xr1.at[1], x_dn),
        planned(ys1.at[1], yr1.at[0], y_up),
        planned(ys1.at[0], yr1.at[1], y_dn),
    ]
    means_sent = [planned(mean, mean_got.at[d], {"gz": column[d]}) for d in range(1, nz)]

    loads = []
    for src, dst in (
        (density_in, density),
        (velocity_in, velocity),
        (pressure_in, pressure),
        (parents_in, parents),
        (shifts_in, shifts),
        (fine_density_in, fine_density),
        (fine_velocity_in, fine_velocity),
        (fine_pressure_in, fine_pressure),
    ):
        load = pltpu.make_async_copy(src, dst, load_sem.at[len(loads)])
        load.start()
        loads.append(load)

    barrier = pltpu.get_barrier_semaphore()
    partners = [x_up, x_dn, y_up, y_dn] + [{"gz": column[d]} for d in range(1, nz)]
    for device in partners:
        pl.semaphore_signal(barrier, inc=1, device_id=device, device_id_type=MESH)

    lane1 = lax.broadcasted_iota(jnp.int32, (8, 128), 1)
    lane3 = lax.broadcasted_iota(jnp.int32, (1, 8, 128), 2)

    def pack_z(fields, at):
        packed = jnp.zeros((4, 8, 128), F32)
        for f in range(5):
            packed = jnp.where(lane3 // 4 == f, roll(fields[f], 2 + 4 * f, 2), packed)
        zs[at] = packed

    def start_halos(fields, at):
        pack_z(fields, at)
        for f in range(5):
            xs[at, 0, f] = fields[f][:, 2:4, :]
            xs[at, 1, f] = fields[f][:, 4:6, :]
            ys[at, 0, f] = fields[f][0:2, 2:6, :]
            ys[at, 1, f] = fields[f][2:4, 2:6, :]
        if at == 0:
            pl.semaphore_wait(barrier, len(partners))
        for copy in halo_copies(at):
            copy.start()

    def coarse_stage(at):
        copies = halo_copies(at)
        for copy in copies[2:6]:
            copy.wait_recv()
        for f in range(5):
            ext[f, 0:2, 2:6, :] = yr[at, 0, f]
            ext[f, 6:8, 2:6, :] = yr[at, 1, f]
        ends = jnp.where(lane3 % 4 < 2, zr[at, 0], zr[at, 1])
        ends = [roll(ends, 126 - 4 * f, 2) for f in range(5)]
        change = coarse_fluxes_yz([ext[f] for f in range(5)], ends)
        for copy in copies[0:2]:
            copy.wait_recv()
        for f in range(5):
            ext[f, 2:6, 0:2, :] = xr[at, 0, f]
            ext[f, 2:6, 6:8, :] = xr[at, 1, f]
        block = [ext[f, 2:6] for f in range(5)]
        change = [a + b for a, b in zip(change, coarse_fluxes_x(block))]
        return block, change

    group = lax.broadcasted_iota(jnp.int32, (48, 128), 1) // 32

    def start_picked(rows, size, out, into, copies):
        for chunk in range((nz + 3) // 4):
            picked = [mm(rows[r], sel[chunk, r]) for r in range(4)]
            for d in range(4 * chunk, min(4 * chunk + 4, nz)):
                body = jnp.zeros((size, 128), F32)
                for r in range(4):
                    body = jnp.where(group[0:size] == (d + r) % 4, picked[r][0:size], body)
                parts = [(0, size, body)]
                total = into.shape[1]
                if total > size:
                    tail = jnp.where(lane1 // 32 == d % 4, picked[0][size:total], 0.0)
                    parts.append((size, total, tail))
                for low, high, part in parts:
                    if d == 0:
                        into[0, low:high, :] = part
                    else:
                        out[d - 1, low:high, :] = part
                if d > 0:
                    copies[d - 1].start()

    def take_picked(copies, into):
        for copy in copies:
            copy.wait_recv()
        total = into[0]
        for d in range(1, nz):
            total = total + roll(into[d], -32 * (d % 4), 1)
        return total

    def tiles(total, count):
        return [total[8 * k : 8 * k + 8] for k in range(count)]

    def turned(first, last):
        return [roll(first, -32 * f, 1) for f in range(4)] + [last]

    row2 = lax.broadcasted_iota(jnp.int32, (8, 128), 0)

    def doubled(tile, base):
        out = tile[base : base + 1]
        for k in range(1, 4):
            out = jnp.where(row2 >= 2 * k, tile[base + k : base + k + 1], out)
        return jnp.broadcast_to(out, (8, 128))

    def both(matrix, first_row, left):
        rows = matrix[first_row : first_row + 8]
        return jnp.stack([rows[:, left : left + 128], rows[:, left + 128 : left + 256]])

    def x_rows(inner):
        out = []
        for at in (1, 6):
            tile = jnp.zeros((8, 128), F32)
            for f in range(5):
                tile = jnp.where(row2 == f, inner[f][at : at + 1], tile)
            out.append(tile)
        return out

    def put_x(matrix, first_row):
        low, high = both(matrix, first_row, 0), both(matrix, first_row + 8, 0)
        for f in range(5):
            rim[0, f] = jnp.where(row3 < 4, low[:, f : f + 1, :], high[:, f : f + 1, :])

    def put_y(faces):
        rows = [doubled(tile, 0) for tile in faces] + [doubled(tile, 4) for tile in faces]
        sides = mm(jnp.concatenate(rows), expand_y[...])
        for f in range(5):
            rim[1, f] = jnp.where(lane3 < 64, both(sides, 8 * f, 0), both(sides, 40 + 8 * f, 0))

    row3 = lax.broadcasted_iota(jnp.int32, (1, 8, 128), 1)

    ext[...] = jnp.ones(ext.shape, F32)
    for load in loads[0:3]:
        load.wait()
    for y in range(4):
        ext[0, 2 + y, 2:6, :] = density[:, y, :]
        for k in range(3):
            ext[1 + k, 2 + y, 2:6, :] = velocity[k, :, y, :]
        ext[4, 2 + y, 2:6, :] = pressure[:, y, :]
    start_halos([ext[f, 2:6] for f in range(5)], 0)
    for load in loads[3:8]:
        load.wait()

    big_row = lax.broadcasted_iota(jnp.int32, (128, 128), 0)

    def one_hot(index):
        return jnp.where(big_row == index[0:1, :], 1.0, 0.0).astype(BF16)

    slot = lane1 % 16
    for chunk in range((nz + 3) // 4):
        target = jnp.full((8, 128), -4 * cz * nz, jnp.int32)
        for d in range(4 * chunk, min(4 * chunk + 4, nz)):
            for b in range(2):
                box = 2 * column[d] + b
                low = parents[box] * cz + shifts[box] - 1
                target = jnp.where(lane1 // 16 == 2 * (d % 4) + b, low + slot, target)
        target = jnp.where(target == -1, target + nz * cz, target)
        target = jnp.where(target >= nz * cz, target - nz * cz, target)
        target = jnp.where(slot < 10, target - gz * cz, -1)
        for r in range(4):
            sel[chunk, r] = one_hot(roll(target, 32 * r, 1))
    fine_y, fine_z = lane1 // 16, lane1 % 16
    for b in range(2):
        base = (fine_y // 2) * 32 + 16 * b
        expand_t[:, 128 * b : 128 * b + 128] = one_hot(base + fine_z // 2 + 1)
        expand_t[:, 256 + 128 * b : 384 + 128 * b] = one_hot(base + jnp.where(fine_z < 8, 0, 9))
        expand_y[:, 128 * b : 128 * b + 128] = one_hot(16 * b + fine_z // 2 + 1)
    big_lane = lax.broadcasted_iota(jnp.int32, (128, 128), 1)
    for pair in range((nz + 1) // 2):
        target = jnp.full((128, 128), -4 * cz, jnp.int32)
        for k in range(2):
            d = 2 * pair + k
            if d < nz:
                owner = column[(nz - d) % nz]
                for b in range(2):
                    box = 2 * owner + b
                    low = jnp.where(parents[box] == gz, shifts[box], -4 * cz)
                    target = jnp.where(big_row // 32 == 2 * k + b, low, target)
        hit = big_lane == target + big_row % 8
        for y in range(4):
            place[128 * pair : 128 * pair + 128, 128 * y : 128 * y + 128] = jnp.where(
                hit & ((big_row % 32) // 8 == y), 1.0, 0.0
            ).astype(BF16)
    count = jnp.zeros((8, 128), F32)
    for box in range(2 * nz):
        low = jnp.where(parents[box] == gz, shifts[box], -4 * cz)
        count = count + jnp.where((lane1 >= low) & (lane1 < low + 8), 1.0, 0.0)
    covered = count[0:4] > 0.0
    share = 1.0 / jnp.maximum(count[0:4], 1.0)

    @pl.loop(0, 2)
    def _(at):
        block, change = coarse_stage(at)
        base = to_conserved(block)
        moved = [a + DT_COARSE * b for a, b in zip(base, change)]

        @pl.when(at == 0)
        def _():
            section = to_primitive(moved)
            start_halos(section, 1)
            for f in range(5):
                upd[f] = base[f]
                yf[f, 0:4, :] = ext[f, 1, 2:6, :]
                yf[f, 4:8, :] = ext[f, 6, 2:6, :]
            rows = []
            for r in range(4):
                rows.append(
                    jnp.concatenate([ext[f, 2 + r] for f in range(5)] + [yf[r], yf[4], yf[4]])
                )
            start_picked(rows, 48, msg, got, windows)
            for f in range(5):
                ext[f, 2:6, 2:6, :] = section[f][:, 2:6, :]

        @pl.when(at == 1)
        def _():
            for f in range(5):
                new = 0.5 * upd[f] + 0.5 * moved[f]
                upd[f] = new
                xs1[0, f] = new[:, 2:3, :]
                xs1[1, f] = new[:, 5:6, :]
                ys1[0, f] = new[0, 2:6, :]
                ys1[1, f] = new[3, 2:6, :]
            for copy in faces_sent:
                copy.start()

    rows = []
    for r in range(4):
        rows.append(jnp.concatenate([upd[f, r] for f in range(5)] + [upd[4, r]]))
    start_picked(rows, 40, msg_z, got_z, near)

    total = take_picked(windows, got)
    old_inner, old_faces = tiles(total, 5), turned(total[40:48], total[48:56])
    for f in range(5):
        win[f] = old_inner[f]
        win[5 + f] = old_faces[f]
    rows = [doubled(tile, 2) for tile in old_inner] + x_rows(old_inner)
    wide = mm(jnp.concatenate(rows + rows[0:1]), expand_t[...])
    detail = [fine_density[...]] + [fine_velocity[k] for k in range(3)] + [fine_pressure[...]]
    first = to_conserved([both(wide, 8 * f, 0) + detail[f] for f in range(5)])
    for f in range(5):
        fine_out[f] = first[f]
        now[f] = first[f]
        rim[2, f] = both(wide, 8 * f, 256)
    put_x(wide, 40)
    put_y(old_faces)

    for copy in faces_sent:
        copy.wait_recv()
    xf[...] = jnp.zeros(xf.shape, F32)
    for f in range(5):
        xf[:, f, :] = xr1[0, f, :, 0, :]
        xf[:, 8 + f, :] = xr1[1, f, :, 0, :]
        yf[f, 0:4, :] = yr1[0, f]
        yf[f, 4:8, :] = yr1[1, f]
    rows = [jnp.concatenate([xf[r], yf[r], yf[4]]) for r in range(4)]
    start_picked(rows, 24, msg_f, got_f, far)

    def middle(old, new):
        mixed = [0.5 * (a + b) for a, b in zip(to_conserved(old), new)]
        mixed[0] = jnp.where(mixed[0] == 0.0, 1.0, mixed[0])
        return to_primitive(mixed)

    @pl.loop(0, 4)
    def _(step):
        current = [now[f] for f in range(5)]
        ghosts = [[rim[axis, f] for f in range(5)] for axis in range(3)]
        rate = fine_tendency(to_primitive(current), ghosts)
        kept = jnp.where(step % 2 == 0, 0.0, 0.5)
        state = [
            kept * fine_out[f] + (1.0 - kept) * (current[f] + DT_FINE * rate[f]) for f in range(5)
        ]
        for f in range(5):
            now[f] = state[f]

        @pl.when(step % 2 == 1)
        def _():
            for f in range(5):
                fine_out[f] = state[f]

        @pl.when(step == 0)
        def _():
            inner = middle([win[f] for f in range(5)], tiles(take_picked(near, got_z), 5))
            rows = [doubled(tile, 2) for tile in inner]
            wide = mm(jnp.concatenate(rows + rows[0:1]), expand_t[:, 256:512])
            for f in range(5):
                rim[3, f] = both(wide, 8 * f, 0)

        @pl.when(step == 1)
        def _():
            total = take_picked(far, got_f)
            put_y(middle([win[5 + f] for f in range(5)], turned(total[16:24], total[24:32])))
            sides = [
                jnp.where(row2 == 1, total[f : f + 1], total[8 + f : 9 + f]) for f in range(5)
            ]
            rows = x_rows(middle([win[f] for f in range(5)], sides))
            put_x(mm(jnp.concatenate(rows), expand_t[:, 0:256]), 0)
            for f in range(5):
                rim[2, f] = rim[3, f]

    state = [now[f] for f in range(5)]

    child = big_row // 32 * 8 + (big_row % 16) // 2
    matrix = jnp.where(big_lane == child, 0.125, 0.0).astype(BF16)
    flat = mm(jnp.concatenate([a[b] for b in range(2) for a in state]), matrix)
    summed = flat[0:40] + roll(flat[40:80], 32, 1)
    summed = summed + roll(summed, -1, 0)
    keep = (row2 % 2 == 0) & (lane1 < 64)
    parts = [jnp.where(keep, tile, 0.0) for tile in tiles(summed, 5)]
    odd = roll(parts[2] + roll(parts[3], 64, 1), 1, 0)
    packed = jnp.concatenate([parts[0] + roll(parts[1], 64, 1) + odd, parts[4]])
    mean[...] = packed
    mean_got[0] = packed
    for copy in means_sent:
        copy.start()
    for copy in means_sent:
        copy.wait_recv()
    rows = []
    for pair in range((nz + 1) // 2):
        here = mean_got[2 * pair]
        there = mean_got[2 * pair + 1] if 2 * pair + 1 < nz else jnp.zeros((16, 128), F32)
        first = jnp.where(lane1 < 64, here[0:8], roll(there[0:8], 64, 1))
        second = jnp.where(lane1 < 64, roll(here[0:8], 64, 1), there[0:8])
        third = jnp.where(lane1 < 64, here[8:16], roll(there[8:16], 64, 1))
        rows.append(jnp.concatenate([first, second, third, third]))
    total = mm(jnp.concatenate(rows, axis=1), place[...])
    for k in range(3):
        for y in range(4):
            laid[k, y] = total[8 * k : 8 * k + 8, 128 * y : 128 * y + 128]
    for f in range(5):
        tile, at = ((0, 0), (1, 0), (0, 1), (1, 1), (2, 0))[f]
        for y in range(4):
            value = laid[tile, y, pl.ds(at, 4, stride=2), :] * share
            coarse_out[f, :, y, :] = jnp.where(covered, value, upd[f, y, 2:6, :])
    for copy in halo_copies(0) + halo_copies(1) + started:
        copy.wait_send()


def on_device(sizes, density, velocity, pressure, fine_density, fine_velocity, fine_pressure, parent, shift):
    nz = sizes[2]
    fine = fine_density.shape[2:]
    vmem = pl.BlockSpec(memory_space=pltpu.VMEM)
    hbm = pl.BlockSpec(memory_space=pltpu.HBM)
    copies = 16 + 4 * (nz - 1)
    chunks = (nz + 3) // 4
    scratch = [
        density.shape,
        velocity.shape,
        pressure.shape,
        fine,
        (3,) + fine,
        fine,
        (5, 8, 8, 128),
        (2, 2, 5, 4, 2, 128),
        (2, 2, 5, 4, 2, 128),
        (2, 2, 5, 2, 4, 128),
        (2, 2, 5, 2, 4, 128),
        (2, 4, 8, 128),
        (2, 2, 4, 8, 128),
        (2, 5, 4, 1, 128),
        (2, 5, 4, 1, 128),
        (2, 5, 4, 128),
        (2, 5, 4, 128),
        (5, 8, 128),
        (4, 16, 128),
        (nz - 1, 56, 128),
        (nz, 56, 128),
        (nz - 1, 40, 128),
        (nz, 40, 128),
        (nz - 1, 32, 128),
        (nz, 32, 128),
        (16, 128),
        (nz, 16, 128),
        (3, 4, 8, 128),
        (5, 4, 8, 128),
        (10, 8, 128),
        (4, 5) + fine,
        (5,) + fine,
    ]
    matrices = [(chunks, 4, 128, 128), (128, 512), (128, 256), (128 * ((nz + 1) // 2), 512)]
    coarse, fine_state = pl.pallas_call(
        functools.partial(kernel, sizes),
        out_shape=(
            pltpu.VMEM((5,) + density.shape, F32),
            pltpu.VMEM((5,) + fine, F32),
        ),
        in_specs=[hbm] * 8,
        out_specs=(vmem, vmem),
        scratch_shapes=[pltpu.VMEM(shape, F32) for shape in scratch]
        + [pltpu.VMEM(shape, BF16) for shape in matrices]
        + [pltpu.SMEM((2 * nz,), jnp.int32)] * 2
        + [pltpu.SemaphoreType.DMA((8,)), pltpu.SemaphoreType.DMA((copies,)), pltpu.SemaphoreType.DMA((copies,))],
        compiler_params=pltpu.CompilerParams(
            collective_id=0, has_side_effects=True, vmem_limit_bytes=56 * 1024 * 1024
        ),
    )(
        density,
        velocity,
        pressure,
        fine_density.reshape(fine),
        fine_velocity.reshape((3,) + fine),
        fine_pressure.reshape(fine),
        parent.reshape(-1),
        shift.reshape(-1),
    )
    return coarse, fine_state.reshape((5, 1, 1) + fine)


def solution(mesh):
    sizes = tuple(mesh.shape[axis] for axis in ("gx", "gy", "gz"))
    in_specs = (
        P("gx", "gy", "gz"),
        P(None, "gx", "gy", "gz"),
        P("gx", "gy", "gz"),
        P("gx", "gy", "gz", None, None),
        P(None, "gx", "gy", "gz", None, None),
        P("gx", "gy", "gz", None, None),
        P("gx", "gy", None, None),
        P("gx", "gy", None),
    )
    out_specs = (P(None, "gx", "gy", "gz"), P(None, "gx", "gy", "gz", None, None))
    return jax.shard_map(
        functools.partial(on_device, sizes),
        mesh=mesh,
        in_specs=in_specs,
        out_specs=out_specs,
        check_vma=False,
    )
```

```python
import functools

import jax
import jax.numpy as jnp
from jax import lax
from jax.experimental import pallas as pl
from jax.experimental.pallas import tpu as pltpu
from jax.sharding import PartitionSpec as P

GAMMA = 1.4
DT_COARSE = 0.05
DT_FINE = 0.025
TINY = 1e-30
MESH = pl.DeviceIdType.MESH
F32 = jnp.float32
BF16 = jnp.bfloat16


def mm(a, b):
    size = a.shape[0]
    high = a.astype(BF16).astype(F32)
    rest = a - high
    middle = rest.astype(BF16).astype(F32)
    parts = jnp.concatenate([high, middle, rest - middle]).astype(BF16)
    out = lax.dot_general(parts, b, (((1,), (0,)), ((), ())), preferred_element_type=F32)
    return (out[0:size] + out[size : 2 * size]) + out[2 * size : 3 * size]


def inverse(a):
    near = pl.reciprocal(a, approx=True)
    return near * (2.0 - a * near)


def to_conserved(q):
    rho, u, v, w, p = q
    energy = p * (1.0 / (GAMMA - 1.0)) + 0.5 * rho * (u * u + v * v + w * w)
    return [rho, rho * u, rho * v, rho * w, energy]


def to_primitive(c):
    rho, mx, my, mz, energy = c
    inv = inverse(rho)
    u, v, w = mx * inv, my * inv, mz * inv
    p = (GAMMA - 1.0) * (energy - 0.5 * (mx * u + my * v + mz * w))
    return [rho, u, v, w, p]


def minmod(a, b):
    return jnp.maximum(jnp.minimum(a, b), 0.0) + jnp.minimum(jnp.maximum(a, b), 0.0)


def hllc(left, right):
    rl, ul, _, _, pl_ = left
    rr, ur, _, _, pr = right
    sound_l = GAMMA * pl_ * inverse(rl)
    sound_r = GAMMA * pr * inverse(rr)
    cl = sound_l * lax.rsqrt(jnp.maximum(sound_l, TINY))
    cr = sound_r * lax.rsqrt(jnp.maximum(sound_r, TINY))
    sl = jnp.minimum(ul - cl, ur - cr)
    sr = jnp.maximum(ul + cl, ur + cr)
    ml = rl * (sl - ul)
    mr = rr * (sr - ur)
    contact = (pr - pl_ + ml * ul - mr * ur) * inverse(ml - mr)
    use_left = (sl >= 0.0) | (contact >= 0.0)
    rho, un, t1, t2, p = [jnp.where(use_left, a, b) for a, b in zip(left, right)]
    wave = jnp.where(use_left, sl, sr)
    mass = jnp.where(use_left, ml, mr)
    outside = (sl >= 0.0) | (jnp.logical_not(use_left) & (sr < 0.0))
    scale = inverse(wave - contact)
    energy = p * (1.0 / (GAMMA - 1.0)) + 0.5 * rho * (un * un + t1 * t1 + t2 * t2)
    star_rho = mass * scale
    star_energy = ((wave - un) * energy + (contact - un) * (mass * contact + p)) * scale
    flow = rho * un
    zero = jnp.zeros_like(rho)
    f0 = flow + jnp.where(outside, zero, wave * (star_rho - rho))
    fn = flow * un + p + jnp.where(outside, zero, wave * (star_rho * contact - flow))
    fe = (energy + p) * un + jnp.where(outside, zero, wave * (star_energy - energy))
    return [f0, fn, t1 * f0, t2 * f0, fe]


TURN = ((0, 1, 2, 3, 4), (0, 2, 3, 1, 4), (0, 3, 1, 2, 4))


def stacked_flux(lefts, rights):
    sizes = [part[0].shape[0] for _, part in lefts]

    def joined(parts):
        return [jnp.concatenate([part[TURN[axis][i]] for axis, part in parts]) for i in range(5)]

    fluxes = hllc(joined(lefts), joined(rights))
    out = []
    at = 0
    for (axis, _), size in zip(lefts, sizes):
        part = [None] * 5
        for i in range(5):
            part[TURN[axis][i]] = fluxes[i][at : at + size]
        out.append(part)
        at += size
    return out


def roll(a, shift, axis):
    size = a.shape[axis]
    shift = shift % size
    return a if shift == 0 else pltpu.roll(a, shift, axis)


def coarse_fluxes_yz(q, n):
    lane = lax.broadcasted_iota(jnp.int32, (1, 8, 128), 2)
    row = lax.broadcasted_iota(jnp.int32, (1, 8, 128), 1)
    inner = (row >= 2) & (row < 6)
    ly, ry, lz, rz = [], [], [], []
    for f in range(5):
        a = q[f]
        jump = a[1:8] - a[0:7]
        half = 0.5 * minmod(jump[0:6], jump[1:7])
        ly.append(a[1:6] + half[0:5])
        ry.append(a[2:7] - half[1:6])
        c = a[2:6]
        g = n[f]
        before = roll(jnp.where(lane == 127, g, c), 1, 2)
        after = roll(jnp.where(lane == 0, g, c), -1, 2)
        half = 0.5 * minmod(c - before, after - c)
        g_before = roll(jnp.where(lane == 127, c, g), 1, 2)
        g_after = roll(jnp.where(lane == 0, c, g), -1, 2)
        g_half = 0.5 * minmod(g - g_before, g_after - g)
        up = c + half
        down = c - half
        low_left = roll(jnp.where(lane == 127, g + g_half, up), 1, 2)
        high_right = roll(jnp.where(lane == 0, g - g_half, down), -1, 2)
        lz.append(jnp.where(inner, low_left, roll(up, 4, 1)))
        rz.append(jnp.where(inner, down, roll(high_right, 4, 1)))
    fy, fz = stacked_flux([(1, ly), (2, lz)], [(1, ry), (2, rz)])
    out = []
    for f in range(5):
        dy = fy[f][1:5] - fy[f][0:4]
        dz = roll(fz[f], 4, 1) - fz[f]
        out.append(-dy - dz)
    return out


def coarse_fluxes_x(q):
    lx, rx = [], []
    for c in q:
        jump = c - roll(c, 1, 1)
        half = 0.5 * minmod(jump, roll(jump, -1, 1))
        lx.append(roll(c + half, 1, 1))
        rx.append(c - half)
    (fx,) = stacked_flux([(0, lx)], [(0, rx)])
    return [a - roll(a, -1, 1) for a in fx]


def fine_tendency(q, ghosts):
    lane = lax.broadcasted_iota(jnp.int32, (1, 8, 128), 2)
    row = lax.broadcasted_iota(jnp.int32, (1, 8, 128), 1)
    firsts = (row == 0, lane < 16, lane % 16 == 0)
    lasts = (row == 7, lane >= 112, lane % 16 == 15)
    steps = ((1, 1), (16, 2), (1, 2))
    moves = ((4, 1), (64, 2), (8, 2))
    halves = (row >= 4, lane >= 64, lane % 16 >= 8)

    def shared(fields, axis):
        move, dim = moves[axis]
        return [jnp.where(halves[axis], a[0:1], roll(a[1:2], move, dim)) for a in fields]

    lefts, rights, end_lefts, end_rights = [], [], [], []
    for axis in range(3):
        step, dim = steps[axis]
        left, right, tops = [], [], []
        for f in range(5):
            a = q[f]
            g = ghosts[axis][f]
            before = jnp.where(firsts[axis], g, roll(a, step, dim))
            after = jnp.where(lasts[axis], g, roll(a, -step, dim))
            half = 0.5 * minmod(a - before, after - a)
            up = a + half
            left.append(jnp.where(firsts[axis], g, roll(up, step, dim)))
            right.append(a - half)
            tops.append(up)
        lefts.append((axis, left))
        rights.append((axis, right))
        end_lefts.append((axis, shared(tops, axis)))
        end_rights.append((axis, shared(ghosts[axis], axis)))
    parts = stacked_flux(lefts + end_lefts, rights + end_rights)
    out = [None] * 5
    for axis in range(3):
        step, dim = steps[axis]
        for f in range(5):
            low = parts[axis][f]
            top = parts[3 + axis][f]
            top = jnp.concatenate([top, roll(top, -moves[axis][0], dim)])
            change = jnp.where(lasts[axis], top, roll(low, -step, dim)) - low
            out[f] = -change if out[f] is None else out[f] - change
    return [2.0 * part for part in out]


def kernel(
    sizes,
    density_in,
    velocity_in,
    pressure_in,
    fine_density_in,
    fine_velocity_in,
    fine_pressure_in,
    parents_in,
    shifts_in,
    coarse_out,
    fine_out,
    density,
    velocity,
    pressure,
    fine_density,
    fine_velocity,
    fine_pressure,
    ext,
    xs,
    xr,
    ys,
    yr,
    zs,
    zr,
    xs1,
    xr1,
    ys1,
    yr1,
    yf,
    xf,
    msg,
    got,
    msg_z,
    got_z,
    msg_f,
    got_f,
    mean,
    mean_got,
    laid,
    upd,
    win,
    rim,
    now,
    sel,
    expand_t,
    expand_y,
    place,
    parents,
    shifts,
    load_sem,
    send_sem,
    recv_sem,
):
    nx, ny, nz = sizes
    cz = 128
    gx, gy, gz = lax.axis_index("gx"), lax.axis_index("gy"), lax.axis_index("gz")
    x_up, x_dn = {"gx": lax.rem(gx + 1, nx)}, {"gx": lax.rem(gx + nx - 1, nx)}
    y_up, y_dn = {"gy": lax.rem(gy + 1, ny)}, {"gy": lax.rem(gy + ny - 1, ny)}
    column = [lax.rem(gz + d, nz) for d in range(nz)]
    z_up, z_dn = {"gz": column[1]}, {"gz": column[nz - 1]}
    started = []

    def remote(src, dst, device, at):
        return pltpu.make_async_remote_copy(
            src_ref=src,
            dst_ref=dst,
            send_sem=send_sem.at[at],
            recv_sem=recv_sem.at[at],
            device_id=device,
            device_id_type=MESH,
        )

    def planned(src, dst, device):
        copy = remote(src, dst, device, 12 + len(started))
        started.append(copy)
        return copy

    def halo_copies(at):
        pairs = [
            (xs.at[at, 1], xr.at[at, 0], x_up),
            (xs.at[at, 0], xr.at[at, 1], x_dn),
            (ys.at[at, 1], yr.at[at, 0], y_up),
            (ys.at[at, 0], yr.at[at, 1], y_dn),
            (zs.at[at], zr.at[at, 0], z_up),
            (zs.at[at], zr.at[at, 1], z_dn),
        ]
        return [remote(*pair, 6 * at + k) for k, pair in enumerate(pairs)]

    def to_column(out, into):
        return [planned(out.at[d - 1], into.at[d], {"gz": column[d]}) for d in range(1, nz)]

    windows, near, far = to_column(msg, got), to_column(msg_z, got_z), to_column(msg_f, got_f)
    faces_sent = [
        planned(xs1.at[1], xr1.at[0], x_up),
        planned(xs1.at[0], xr1.at[1], x_dn),
        planned(ys1.at[1], yr1.at[0], y_up),
        planned(ys1.at[0], yr1.at[1], y_dn),
    ]
    means_sent = [planned(mean, mean_got.at[d], {"gz": column[d]}) for d in range(1, nz)]

    loads = []
    for src, dst in (
        (density_in, density),
        (velocity_in, velocity),
        (pressure_in, pressure),
        (parents_in, parents),
        (shifts_in, shifts),
        (fine_density_in, fine_density),
        (fine_velocity_in, fine_velocity),
        (fine_pressure_in, fine_pressure),
    ):
        load = pltpu.make_async_copy(src, dst, load_sem.at[len(loads)])
        load.start()
        loads.append(load)

    barrier = pltpu.get_barrier_semaphore()
    partners = [x_up, x_dn, y_up, y_dn] + [{"gz": column[d]} for d in range(1, nz)]
    for device in partners:
        pl.semaphore_signal(barrier, inc=1, device_id=device, device_id_type=MESH)

    lane1 = lax.broadcasted_iota(jnp.int32, (8, 128), 1)
    lane3 = lax.broadcasted_iota(jnp.int32, (1, 8, 128), 2)

    def pack_z(fields, at):
        packed = jnp.zeros((4, 8, 128), F32)
        for f in range(5):
            packed = jnp.where(lane3 // 4 == f, roll(fields[f], 2 + 4 * f, 2), packed)
        zs[at] = packed

    def start_halos(fields, at):
        pack_z(fields, at)
        for f in range(5):
            for y in range(4):
                xs[at, 0, f, 2 * y : 2 * y + 2, :] = fields[f][y, 2:4, :]
                xs[at, 1, f, 2 * y : 2 * y + 2, :] = fields[f][y, 4:6, :]
            for k in range(2):
                ys[at, 0, f, 4 * k : 4 * k + 4, :] = fields[f][k, 2:6, :]
                ys[at, 1, f, 4 * k : 4 * k + 4, :] = fields[f][2 + k, 2:6, :]
        if at == 0:
            pl.semaphore_wait(barrier, len(partners))
        for copy in halo_copies(at):
            copy.start()

    def coarse_stage(at):
        copies = halo_copies(at)
        for copy in copies[2:6]:
            copy.wait_recv()
        for f in range(5):
            for k in range(2):
                ext[f, k, 2:6, :] = yr[at, 0, f, 4 * k : 4 * k + 4, :]
                ext[f, 6 + k, 2:6, :] = yr[at, 1, f, 4 * k : 4 * k + 4, :]
        ends = jnp.where(lane3 % 4 < 2, zr[at, 0], zr[at, 1])
        ends = [roll(ends, 126 - 4 * f, 2) for f in range(5)]
        change = coarse_fluxes_yz([ext[f] for f in range(5)], ends)
        for copy in copies[0:2]:
            copy.wait_recv()
        for f in range(5):
            for y in range(4):
                ext[f, 2 + y, 0:2, :] = xr[at, 0, f, 2 * y : 2 * y + 2, :]
                ext[f, 2 + y, 6:8, :] = xr[at, 1, f, 2 * y : 2 * y + 2, :]
        block = [ext[f, 2:6] for f in range(5)]
        change = [a + b for a, b in zip(change, coarse_fluxes_x(block))]
        return block, change

    group = lax.broadcasted_iota(jnp.int32, (48, 128), 1) // 32

    def start_picked(rows, size, out, into, copies):
        for chunk in range((nz + 3) // 4):
            picked = [mm(rows[r], sel[chunk, r]) for r in range(4)]
            for d in range(4 * chunk, min(4 * chunk + 4, nz)):
                body = jnp.zeros((size, 128), F32)
                for r in range(4):
                    body = jnp.where(group[0:size] == (d + r) % 4, picked[r][0:size], body)
                parts = [(0, size, body)]
                total = into.shape[1]
                if total > size:
                    tail = jnp.where(lane1 // 32 == d % 4, picked[0][size:total], 0.0)
                    parts.append((size, total, tail))
                for low, high, part in parts:
                    if d == 0:
                        into[0, low:high, :] = part
                    else:
                        out[d - 1, low:high, :] = part
                if d > 0:
                    copies[d - 1].start()

    def take_picked(copies, into):
        for copy in copies:
            copy.wait_recv()
        total = into[0]
        for d in range(1, nz):
            total = total + roll(into[d], -32 * (d % 4), 1)
        return total

    def tiles(total, count):
        return [total[8 * k : 8 * k + 8] for k in range(count)]

    def turned(first, last):
        return [roll(first, -32 * f, 1) for f in range(4)] + [last]

    row2 = lax.broadcasted_iota(jnp.int32, (8, 128), 0)

    def doubled(tile, base):
        out = tile[base : base + 1]
        for k in range(1, 4):
            out = jnp.where(row2 >= 2 * k, tile[base + k : base + k + 1], out)
        return jnp.broadcast_to(out, (8, 128))

    def both(matrix, first_row, left):
        rows = matrix[first_row : first_row + 8]
        return jnp.stack([rows[:, left : left + 128], rows[:, left + 128 : left + 256]])

    def x_rows(inner):
        out = []
        for at in (1, 6):
            tile = jnp.zeros((8, 128), F32)
            for f in range(5):
                tile = jnp.where(row2 == f, inner[f][at : at + 1], tile)
            out.append(tile)
        return out

    def put_x(matrix, first_row):
        low, high = both(matrix, first_row, 0), both(matrix, first_row + 8, 0)
        for f in range(5):
            rim[0, f] = jnp.where(row3 < 4, low[:, f : f + 1, :], high[:, f : f + 1, :])

    def put_y(faces):
        rows = [doubled(tile, 0) for tile in faces] + [doubled(tile, 4) for tile in faces]
        sides = mm(jnp.concatenate(rows), expand_y[...])
        for f in range(5):
            rim[1, f] = jnp.where(lane3 < 64, both(sides, 8 * f, 0), both(sides, 40 + 8 * f, 0))

    row3 = lax.broadcasted_iota(jnp.int32, (1, 8, 128), 1)

    ext[...] = jnp.ones(ext.shape, F32)
    for load in loads[0:3]:
        load.wait()
    for y in range(4):
        ext[0, 2 + y, 2:6, :] = density[:, y, :]
        for k in range(3):
            ext[1 + k, 2 + y, 2:6, :] = velocity[k, :, y, :]
        ext[4, 2 + y, 2:6, :] = pressure[:, y, :]
    start_halos([ext[f, 2:6] for f in range(5)], 0)
    for load in loads[3:8]:
        load.wait()

    big_row = lax.broadcasted_iota(jnp.int32, (128, 128), 0)

    def one_hot(index):
        return jnp.where(big_row == index[0:1, :], 1.0, 0.0).astype(BF16)

    slot = lane1 % 16
    for chunk in range((nz + 3) // 4):
        target = jnp.full((8, 128), -4 * cz * nz, jnp.int32)
        for d in range(4 * chunk, min(4 * chunk + 4, nz)):
            for b in range(2):
                box = 2 * column[d] + b
                low = parents[box] * cz + shifts[box] - 1
                target = jnp.where(lane1 // 16 == 2 * (d % 4) + b, low + slot, target)
        target = jnp.where(target == -1, target + nz * cz, target)
        target = jnp.where(target >= nz * cz, target - nz * cz, target)
        target = jnp.where(slot < 10, target - gz * cz, -1)
        for r in range(4):
            sel[chunk, r] = one_hot(roll(target, 32 * r, 1))
    fine_y, fine_z = lane1 // 16, lane1 % 16
    for b in range(2):
        base = (fine_y // 2) * 32 + 16 * b
        expand_t[:, 128 * b : 128 * b + 128] = one_hot(base + fine_z // 2 + 1)
        expand_t[:, 256 + 128 * b : 384 + 128 * b] = one_hot(base + jnp.where(fine_z < 8, 0, 9))
        expand_y[:, 128 * b : 128 * b + 128] = one_hot(16 * b + fine_z // 2 + 1)
    big_lane = lax.broadcasted_iota(jnp.int32, (128, 128), 1)
    for pair in range((nz + 1) // 2):
        target = jnp.full((128, 128), -4 * cz, jnp.int32)
        for k in range(2):
            d = 2 * pair + k
            if d < nz:
                owner = column[(nz - d) % nz]
                for b in range(2):
                    box = 2 * owner + b
                    low = jnp.where(parents[box] == gz, shifts[box], -4 * cz)
                    target = jnp.where(big_row // 32 == 2 * k + b, low, target)
        hit = big_lane == target + big_row % 8
        for y in range(4):
            place[128 * pair : 128 * pair + 128, 128 * y : 128 * y + 128] = jnp.where(
                hit & ((big_row % 32) // 8 == y), 1.0, 0.0
            ).astype(BF16)
    count = jnp.zeros((8, 128), F32)
    for box in range(2 * nz):
        low = jnp.where(parents[box] == gz, shifts[box], -4 * cz)
        count = count + jnp.where((lane1 >= low) & (lane1 < low + 8), 1.0, 0.0)
    covered = count[0:4] > 0.0
    share = 1.0 / jnp.maximum(count[0:4], 1.0)

    @pl.loop(0, 2)
    def _(at):
        block, change = coarse_stage(at)
        base = to_conserved(block)
        moved = [a + DT_COARSE * b for a, b in zip(base, change)]

        @pl.when(at == 0)
        def _():
            section = to_primitive(moved)
            start_halos(section, 1)
            for f in range(5):
                upd[f] = base[f]
                yf[f, 0:4, :] = ext[f, 1, 2:6, :]
                yf[f, 4:8, :] = ext[f, 6, 2:6, :]
            rows = []
            for r in range(4):
                rows.append(
                    jnp.concatenate([ext[f, 2 + r] for f in range(5)] + [yf[r], yf[4], yf[4]])
                )
            start_picked(rows, 48, msg, got, windows)
            for f in range(5):
                ext[f, 2:6, 2:6, :] = section[f][:, 2:6, :]

        @pl.when(at == 1)
        def _():
            for f in range(5):
                new = 0.5 * upd[f] + 0.5 * moved[f]
                upd[f] = new
                for y in range(4):
                    xs1[0, 4 * f + y : 4 * f + y + 1, :] = new[y, 2:3, :]
                    xs1[1, 4 * f + y : 4 * f + y + 1, :] = new[y, 5:6, :]
                ys1[0, 4 * f : 4 * f + 4, :] = new[0, 2:6, :]
                ys1[1, 4 * f : 4 * f + 4, :] = new[3, 2:6, :]
            for copy in faces_sent:
                copy.start()

    rows = []
    for r in range(4):
        rows.append(jnp.concatenate([upd[f, r] for f in range(5)] + [upd[4, r]]))
    start_picked(rows, 40, msg_z, got_z, near)

    total = take_picked(windows, got)
    old_inner, old_faces = tiles(total, 5), turned(total[40:48], total[48:56])
    for f in range(5):
        win[f] = old_inner[f]
        win[5 + f] = old_faces[f]
    rows = [doubled(tile, 2) for tile in old_inner] + x_rows(old_inner)
    wide = mm(jnp.concatenate(rows + rows[0:1]), expand_t[...])
    detail = [fine_density[...]] + [fine_velocity[k] for k in range(3)] + [fine_pressure[...]]
    first = to_conserved([both(wide, 8 * f, 0) + detail[f] for f in range(5)])
    for f in range(5):
        fine_out[f] = first[f]
        now[f] = first[f]
        rim[2, f] = both(wide, 8 * f, 256)
    put_x(wide, 40)
    put_y(old_faces)

    for copy in faces_sent:
        copy.wait_recv()
    xf[...] = jnp.zeros(xf.shape, F32)
    for f in range(5):
        xf[:, f, :] = xr1[0, 4 * f : 4 * f + 4, :]
        xf[:, 8 + f, :] = xr1[1, 4 * f : 4 * f + 4, :]
        yf[f, 0:4, :] = yr1[0, 4 * f : 4 * f + 4, :]
        yf[f, 4:8, :] = yr1[1, 4 * f : 4 * f + 4, :]
    rows = [jnp.concatenate([xf[r], yf[r], yf[4]]) for r in range(4)]
    start_picked(rows, 24, msg_f, got_f, far)

    def middle(old, new):
        mixed = [0.5 * (a + b) for a, b in zip(to_conserved(old), new)]
        mixed[0] = jnp.where(mixed[0] == 0.0, 1.0, mixed[0])
        return to_primitive(mixed)

    @pl.loop(0, 4)
    def _(step):
        current = [now[f] for f in range(5)]
        ghosts = [[rim[axis, f] for f in range(5)] for axis in range(3)]
        rate = fine_tendency(to_primitive(current), ghosts)
        kept = jnp.where(step % 2 == 0, 0.0, 0.5)
        state = [
            kept * fine_out[f] + (1.0 - kept) * (current[f] + DT_FINE * rate[f]) for f in range(5)
        ]
        for f in range(5):
            now[f] = state[f]

        @pl.when(step % 2 == 1)
        def _():
            for f in range(5):
                fine_out[f] = state[f]

        @pl.when(step == 0)
        def _():
            inner = middle([win[f] for f in range(5)], tiles(take_picked(near, got_z), 5))
            rows = [doubled(tile, 2) for tile in inner]
            wide = mm(jnp.concatenate(rows + rows[0:1]), expand_t[:, 256:512])
            for f in range(5):
                rim[3, f] = both(wide, 8 * f, 0)

        @pl.when(step == 1)
        def _():
            total = take_picked(far, got_f)
            put_y(middle([win[5 + f] for f in range(5)], turned(total[16:24], total[24:32])))
            sides = [
                jnp.where(row2 == 1, total[f : f + 1], total[8 + f : 9 + f]) for f in range(5)
            ]
            rows = x_rows(middle([win[f] for f in range(5)], sides))
            put_x(mm(jnp.concatenate(rows), expand_t[:, 0:256]), 0)
            for f in range(5):
                rim[2, f] = rim[3, f]

    state = [now[f] for f in range(5)]

    child = big_row // 32 * 8 + (big_row % 16) // 2
    matrix = jnp.where(big_lane == child, 0.125, 0.0).astype(BF16)
    flat = mm(jnp.concatenate([a[b] for b in range(2) for a in state]), matrix)
    summed = flat[0:40] + roll(flat[40:80], 32, 1)
    summed = summed + roll(summed, -1, 0)
    keep = (row2 % 2 == 0) & (lane1 < 64)
    parts = [jnp.where(keep, tile, 0.0) for tile in tiles(summed, 5)]
    odd = roll(parts[2] + roll(parts[3], 64, 1), 1, 0)
    packed = jnp.concatenate([parts[0] + roll(parts[1], 64, 1) + odd, parts[4]])
    mean[...] = packed
    mean_got[0] = packed
    for copy in means_sent:
        copy.start()
    for copy in means_sent:
        copy.wait_recv()
    rows = []
    for pair in range((nz + 1) // 2):
        here = mean_got[2 * pair]
        there = mean_got[2 * pair + 1] if 2 * pair + 1 < nz else jnp.zeros((16, 128), F32)
        first = jnp.where(lane1 < 64, here[0:8], roll(there[0:8], 64, 1))
        second = jnp.where(lane1 < 64, roll(here[0:8], 64, 1), there[0:8])
        third = jnp.where(lane1 < 64, here[8:16], roll(there[8:16], 64, 1))
        rows.append(jnp.concatenate([first, second, third, third]))
    total = mm(jnp.concatenate(rows, axis=1), place[...])
    for k in range(3):
        for y in range(4):
            laid[k, y] = total[8 * k : 8 * k + 8, 128 * y : 128 * y + 128]
    for f in range(5):
        tile, at = ((0, 0), (1, 0), (0, 1), (1, 1), (2, 0))[f]
        for y in range(4):
            value = laid[tile, y, pl.ds(at, 4, stride=2), :] * share
            coarse_out[f, :, y, :] = jnp.where(covered, value, upd[f, y, 2:6, :])
    for copy in halo_copies(0) + halo_copies(1) + started:
        copy.wait_send()


def on_device(sizes, density, velocity, pressure, fine_density, fine_velocity, fine_pressure, parent, shift):
    nz = sizes[2]
    fine = fine_density.shape[2:]
    vmem = pl.BlockSpec(memory_space=pltpu.VMEM)
    hbm = pl.BlockSpec(memory_space=pltpu.HBM)
    copies = 16 + 4 * (nz - 1)
    chunks = (nz + 3) // 4
    scratch = [
        density.shape,
        velocity.shape,
        pressure.shape,
        fine,
        (3,) + fine,
        fine,
        (5, 8, 8, 128),
        (2, 2, 5, 8, 128),
        (2, 2, 5, 8, 128),
        (2, 2, 5, 8, 128),
        (2, 2, 5, 8, 128),
        (2, 4, 8, 128),
        (2, 2, 4, 8, 128),
        (2, 20, 128),
        (2, 20, 128),
        (2, 20, 128),
        (2, 20, 128),
        (5, 8, 128),
        (4, 16, 128),
        (nz - 1, 56, 128),
        (nz, 56, 128),
        (nz - 1, 40, 128),
        (nz, 40, 128),
        (nz - 1, 32, 128),
        (nz, 32, 128),
        (16, 128),
        (nz, 16, 128),
        (3, 4, 8, 128),
        (5, 4, 8, 128),
        (10, 8, 128),
        (4, 5) + fine,
        (5,) + fine,
    ]
    matrices = [(chunks, 4, 128, 128), (128, 512), (128, 256), (128 * ((nz + 1) // 2), 512)]
    coarse, fine_state = pl.pallas_call(
        functools.partial(kernel, sizes),
        out_shape=(
            pltpu.VMEM((5,) + density.shape, F32),
            pltpu.VMEM((5,) + fine, F32),
        ),
        in_specs=[hbm] * 8,
        out_specs=(vmem, vmem),
        scratch_shapes=[pltpu.VMEM(shape, F32) for shape in scratch]
        + [pltpu.VMEM(shape, BF16) for shape in matrices]
        + [pltpu.SMEM((2 * nz,), jnp.int32)] * 2
        + [pltpu.SemaphoreType.DMA((8,)), pltpu.SemaphoreType.DMA((copies,)), pltpu.SemaphoreType.DMA((copies,))],
        compiler_params=pltpu.CompilerParams(
            collective_id=0, has_side_effects=True, vmem_limit_bytes=56 * 1024 * 1024
        ),
    )(
        density,
        velocity,
        pressure,
        fine_density.reshape(fine),
        fine_velocity.reshape((3,) + fine),
        fine_pressure.reshape(fine),
        parent.reshape(-1),
        shift.reshape(-1),
    )
    return coarse, fine_state.reshape((5, 1, 1) + fine)


def solution(mesh):
    sizes = tuple(mesh.shape[axis] for axis in ("gx", "gy", "gz"))
    in_specs = (
        P("gx", "gy", "gz"),
        P(None, "gx", "gy", "gz"),
        P("gx", "gy", "gz"),
        P("gx", "gy", "gz", None, None),
        P(None, "gx", "gy", "gz", None, None),
        P("gx", "gy", "gz", None, None),
        P("gx", "gy", None, None),
        P("gx", "gy", None),
    )
    out_specs = (P(None, "gx", "gy", "gz"), P(None, "gx", "gy", "gz", None, None))
    return jax.shard_map(
        functools.partial(on_device, sizes),
        mesh=mesh,
        in_specs=in_specs,
        out_specs=out_specs,
        check_vma=False,
    )
```
